512 devices in a mesh: dp: 16 (over z), expert: 8 (over y_lo, x), tensor: 4 (over y_hi, core).
Axes of the slice: x: 4, y: 4 (y_hi: 2, y_lo: 2; y = y_hi * 2 + y_lo), z: 16, core: 2. Of those that a mesh axis runs over, the one named last changes fastest.
Arguments:
- tokens: bfloat16 [16, 2, 352, 2048], P('dp'), may hold values from -6 to 6
- upstream: bfloat16 [16, 2, 352, 7168], P('dp', None, None, ('expert', 'tensor')), may hold values from -2 to 2
- router: float32 [16, 2, 8], replicated, may hold values from 0.05 to 1
- counts: int32 [16], replicated, may hold values from 0 to 2, as said below
- w_gate: bfloat16 [8, 2048, 8, 896], P('expert', 'dp', None, 'tensor'), may hold values from -0.125 to 0.125
- w_up: bfloat16 [8, 2048, 8, 896], P('expert', 'dp', None, 'tensor'), may hold values from -0.125 to 0.125
Outputs:
- tokens_grad: bfloat16 [16, 2, 352, 2048], P('dp', None, ('expert', 'tensor'))
- gate_grad: bfloat16 [8, 2048, 8, 896], P('expert', 'dp', None, 'tensor')
- up_grad: bfloat16 [8, 2048, 8, 896], P('expert', 'dp', None, 'tensor')
The draws below stay inside these ranges and needn't reach their ends.
Inputs may be any that keep to these rules, and one draw needn't show every extreme that they name: The counts sum to 16; one or more groups hold 2 segments, and as many groups hold none.
All inputs are finite; a program needn't handle non-finite values.
Results may differ from the reference program's by a relative error of at most 0.02.
Values may be sent and summed in bfloat16 or wider, within the bound.
A program may use at most 64 MiB of HBM per device.

```python
import math
import jax
import jax.numpy as jnp
from jax import lax

D = 2048
FF = 7168
EXPERTS = 8
SEG_LEN = 352
SEG_MAX = 2
FF_BLOCK = 896
N_DP = 16
N_EXPERT = 8
N_TENSOR = 4


def draw_counts(key, part):
    key = jax.random.fold_in(key, 11)
    first_key, second_key = jax.random.split(key)
    order = jax.random.permutation(first_key, N_DP)
    ranking = jnp.argsort(order)
    paired = jax.random.randint(second_key, (), 1, N_DP // 2 + 1)
    filled = jnp.where(ranking < paired, SEG_MAX, jnp.where(ranking < 2 * paired, 0, 1))
    return filled.astype(jnp.int32)


def block_scale(key, shape, pieces, least, largest):
    factor_of, own = 1.0, jax.random.fold_in(key, 6)
    for axis_at, parts in pieces:
        draws = jnp.exp(jax.random.uniform(jax.random.fold_in(own, axis_at), (parts,), jnp.float32, least / len(pieces), largest / len(pieces)))
        factor_of = factor_of * jnp.repeat(draws, shape[axis_at] // parts).reshape([-1 if axis == axis_at else 1 for axis in range(len(shape))])
    return factor_of


def normal_values(own_key, dims, scale, most, cuts=(), held_as=jnp.bfloat16):
    entries = scale * jax.random.normal(own_key, dims, jnp.float32)
    if cuts:
        entries = entries * block_scale(own_key, dims, cuts, -0.22, 0.18)
    return jnp.clip(entries, -most, most).astype(held_as)


def setup_inputs(seed: int = 0) -> dict:
    keys = jax.random.split(jax.random.key(seed), 7)
    return {
        "tokens": normal_values(keys[0], (N_DP, SEG_MAX, SEG_LEN, D), 1.0, 6.0, ((0, 16),)),
        "upstream": normal_values(keys[1], (N_DP, SEG_MAX, SEG_LEN, FF), 0.15, 2.0, ((0, 16), (3, 32))),
        "router": jnp.clip(jnp.exp(jax.random.uniform(keys[2], (N_DP, SEG_MAX, EXPERTS), jnp.float32, math.log(0.05), math.log(1.0))), 0.05, 1.0),
        "counts": draw_counts(jax.random.fold_in(keys[6], 71), 0),
        "w_gate": normal_values(keys[4], (EXPERTS, D, N_EXPERT, FF_BLOCK), D ** -0.5, 0.125, ((0, 8), (1, 16), (3, 4))),
        "w_up": normal_values(keys[5], (EXPERTS, D, N_EXPERT, FF_BLOCK), D ** -0.5, 0.125, ((0, 8), (1, 16), (3, 4))),
    }


def reference(tokens, upstream, router, counts, w_gate, w_up):
    blocks = N_EXPERT * N_TENSOR
    gate_full = w_gate.reshape(EXPERTS, D, FF)
    up_full = w_up.reshape(EXPERTS, D, FF)
    slot_ids = jnp.arange(SEG_MAX, dtype=jnp.int32)
    live_slots = (slot_ids[None, :] < counts[:, None]).reshape(-1)
    flat_tokens = tokens.reshape(N_DP * SEG_MAX, SEG_LEN, D)
    flat_upstream = upstream.reshape(N_DP * SEG_MAX, SEG_LEN, FF)
    flat_router = router.reshape(N_DP * SEG_MAX, EXPERTS)

    def merge_experts(mixing, weights):
        merged_sum = jnp.zeros((D, FF), jnp.float32)
        for expert in range(EXPERTS):
            merged_sum = merged_sum + mixing[expert] * weights[expert].astype(jnp.float32)
        return merged_sum.astype(jnp.bfloat16)

    def compute(operands):
        seg_tokens, seg_upstream, mixing = operands
        merged_gate = merge_experts(mixing, gate_full)
        merged_up = merge_experts(mixing, up_full)
        pre_gate = jnp.dot(seg_tokens, merged_gate, preferred_element_type=jnp.float32)
        pre_up = jnp.dot(seg_tokens, merged_up, preferred_element_type=jnp.float32)
        logistic = jax.nn.sigmoid(pre_gate)
        flowing = seg_upstream.astype(jnp.float32)
        grad_gate = (flowing * pre_up * logistic * (1.0 + pre_gate * (1.0 - logistic))).astype(jnp.bfloat16)
        grad_up = (flowing * pre_gate * logistic).astype(jnp.bfloat16)
        gate_blocks = grad_gate.astype(jnp.float32).reshape(SEG_LEN, blocks, FF // blocks)
        up_blocks = grad_up.astype(jnp.float32).reshape(SEG_LEN, blocks, FF // blocks)
        merged_gate_blocks = merged_gate.astype(jnp.float32).reshape(D, blocks, FF // blocks)
        merged_up_blocks = merged_up.astype(jnp.float32).reshape(D, blocks, FF // blocks)
        block_terms = jnp.einsum("lbf,dbf->bld", gate_blocks, merged_gate_blocks)
        block_terms = block_terms + jnp.einsum("lbf,dbf->bld", up_blocks, merged_up_blocks)
        block_terms = lax.optimization_barrier(block_terms.astype(jnp.bfloat16)).astype(jnp.float32)
        token_grad = jnp.sum(block_terms, axis=0).astype(jnp.bfloat16)
        seg_gate_grad = jnp.dot(seg_tokens.T, grad_gate, preferred_element_type=jnp.float32).astype(jnp.bfloat16)
        seg_up_grad = jnp.dot(seg_tokens.T, grad_up, preferred_element_type=jnp.float32).astype(jnp.bfloat16)
        return token_grad, seg_gate_grad, seg_up_grad

    def empty_slot(operands):
        return (jnp.zeros((SEG_LEN, D), jnp.bfloat16), jnp.zeros((D, FF), jnp.bfloat16), jnp.zeros((D, FF), jnp.bfloat16))

    def scan_step(buffers, scan_item):
        acc_gate, acc_up = buffers
        seg_tokens, seg_upstream, mixing, is_live = scan_item
        token_grad, seg_gate_grad, seg_up_grad = lax.cond(is_live, compute, empty_slot, (seg_tokens, seg_upstream, mixing))
        acc_gate = acc_gate + mixing[:, None, None] * seg_gate_grad.astype(jnp.float32)[None]
        acc_up = acc_up + mixing[:, None, None] * seg_up_grad.astype(jnp.float32)[None]
        return (acc_gate, acc_up), token_grad

    start = (jnp.zeros((EXPERTS, D, FF), jnp.float32), jnp.zeros((EXPERTS, D, FF), jnp.float32))
    (acc_gate, acc_up), token_grads = lax.scan(scan_step, start, (flat_tokens, flat_upstream, flat_router, live_slots))
    tokens_grad = token_grads.reshape(N_DP, SEG_MAX, SEG_LEN, D)
    gate_grad = acc_gate.astype(jnp.bfloat16).reshape(EXPERTS, D, N_EXPERT, FF_BLOCK)
    up_grad = acc_up.astype(jnp.bfloat16).reshape(EXPERTS, D, N_EXPERT, FF_BLOCK)
    return tokens_grad, gate_grad, up_grad
```

```python
import functools

import jax
import jax.numpy as jnp
from jax import lax
from jax.experimental import pallas as pl
from jax.experimental.pallas import tpu as pltpu
from jax.sharding import Mesh, PartitionSpec as P

MESH = pl.DeviceIdType.MESH
PLANE = ("y_lo", "x", "y_hi")
EXPERT = ("y_lo", "x")
PIECES = ((0, 48), (48, 48), (96, 48), (144, 32))
PARTS = ((0, 256), (256, 256), (512, 256), (768, 128))
NT = (((1,), (1,)), ((), ()))
TN = (((0,), (0,)), ((), ()))


def ring_kernel(
    n, rv, wx, tok, ups, tg, wg, merged, stage, contrib, inbox, spread, acc,
    rs_send, rs_recv, ag_send, ag_recv,
):
    z = lax.axis_index("dp")
    half = n // 2
    experts = wx.shape[0]
    right, left = lax.rem(z + 1, n), lax.rem(z + n - 1, n)
    towards = (right, left)

    def ahead(way, d):
        return lax.rem(z + d, n) if way == 0 else lax.rem(z + n - d, n)

    def behind(way, d):
        return ahead(1 - way, d)

    barrier = pltpu.get_barrier_semaphore()
    for other in towards:
        pl.semaphore_signal(barrier, inc=1, device_id={"dp": other}, device_id_type=MESH)
    pl.semaphore_wait(barrier, 2)

    def rs_copy(way, d, p, src):
        rows = pl.ds(*PIECES[p])
        return pltpu.make_async_remote_copy(
            src_ref=src.at[rows],
            dst_ref=inbox.at[way, d - 1, rows],
            send_sem=rs_send.at[way, d - 1, p],
            recv_sem=rs_recv.at[way, d - 1, p],
            device_id={"dp": towards[way]},
            device_id_type=MESH,
        )

    def ag_copy(way, d, p, v):
        rows = pl.ds(*PIECES[p])
        return pltpu.make_async_remote_copy(
            src_ref=spread.at[v, rows],
            dst_ref=spread.at[v, rows],
            send_sem=ag_send.at[way, d - 1, p],
            recv_sem=ag_recv.at[way, d - 1, p],
            device_id={"dp": towards[way]},
            device_id_type=MESH,
        )

    def merge(v):
        weights = [rv[v, e] for e in range(experts)]

        def block(i, carry):
            rows = pl.ds(pl.multiple_of(i * 64, 64), 64)
            total = weights[0] * wx[0, rows].astype(jnp.float32)
            for e in range(1, experts):
                total = total + weights[e] * wx[e, rows].astype(jnp.float32)
            merged[v, rows] = total.astype(jnp.bfloat16)
            return carry

        lax.fori_loop(0, wx.shape[1] // 64, block, 0)

    def partial(v):
        return lax.dot_general(tok[v], merged[v], NT, preferred_element_type=jnp.float32)

    def start_pieces(d, way):
        longer = (0, 1) if way == 0 else (2, 3)
        return longer if d == half else tuple(p for p in range(4) if p not in longer)

    far = ahead(0, half)
    merge(far)
    stage[0] = partial(far).astype(jnp.bfloat16)
    for way in (0, 1):
        for p in start_pieces(half, way):
            rs_copy(way, half, p, stage.at[0]).start()
    for way in (0, 1):
        v = ahead(way, half - 1)
        merge(v)
        contrib[(half - 1) % 2, way] = partial(v)
        for p in start_pieces(half - 1, way):
            rows = pl.ds(*PIECES[p])
            stage[1, rows] = contrib[(half - 1) % 2, way, rows].astype(jnp.bfloat16)
            rs_copy(way, half - 1, p, stage.at[1]).start()

    def pass_on(way, d, p):
        rows = pl.ds(*PIECES[p])
        rs_copy(way, d + 1, p, inbox.at[way, d]).wait_recv()
        total = inbox[way, d, rows].astype(jnp.float32) + contrib[lax.rem(d, 2), way, rows]
        inbox[way, d, rows] = total.astype(jnp.bfloat16)
        rs_copy(way, d, p, inbox.at[way, d]).start()

    def prepare(d, i):
        way, second = i // 2, i % 2
        v = ahead(way, d)
        if second:
            contrib[lax.rem(d, 2), way] = partial(v)
        else:
            merge(v)

    for i in range(4):
        if i < 2:
            pass_on(0, half - 1, start_pieces(half, 0)[i])
            pass_on(1, half - 1, start_pieces(half, 1)[i])
        prepare(half - 2, i)

    def rs_step(i, carry):
        d = half - 2 - i
        for i, (up, down) in enumerate(((2, 0), (3, 1), (0, 2), (1, 3))):
            pass_on(0, d, up)
            pass_on(1, d, down)
            prepare(d - 1, i)
        return carry

    lax.fori_loop(0, half - 2, rs_step, 0)

    def gate_part(gate, up, flowing):
        s = jax.nn.sigmoid(gate)
        return (flowing * up * s * (1.0 + gate * (1.0 - s))).astype(jnp.bfloat16)

    def up_part(gate, flowing):
        return (flowing * gate * jax.nn.sigmoid(gate)).astype(jnp.bfloat16)

    for p in range(4):
        rows = pl.ds(*PIECES[p])
        for way in (0, 1):
            rs_copy(way, 1, p, inbox.at[way, 0]).wait_recv()
        pre = (
            inbox[0, 0, rows].astype(jnp.float32)
            + inbox[1, 0, rows].astype(jnp.float32)
            + contrib[0, 0, rows]
        )
        flowing = ups[rows].astype(jnp.float32)
        gate, mixed, up = pre[:, :384], pre[:, 384:512], pre[:, 512:]
        spread[z, rows, :384] = gate_part(gate, up, flowing[:, :384])
        spread[z, rows, 512:] = up_part(gate, flowing[:, :384])
        low = lax.broadcasted_iota(jnp.int32, mixed.shape, 1) < 64
        rolled = pltpu.roll(mixed, 64, 1)
        gate, up = jnp.where(low, mixed, rolled), jnp.where(low, rolled, mixed)
        spread[z, rows, 384:512] = jnp.where(
            low, gate_part(gate, up, flowing[:, 384:]), up_part(gate, flowing[:, 384:])
        )
        for way in (0, 1):
            ag_copy(way, 1, p, z).start()

    acc[...] = jnp.zeros_like(acc)

    def back(owners, i):
        rows, hidden = pl.ds(*PIECES[i]), pl.ds(*PARTS[i])
        terms = []
        for v in owners:
            tg[v, rows] = jnp.dot(
                spread[v, rows], merged[v], preferred_element_type=jnp.float32
            ).astype(jnp.bfloat16)
            terms.append(
                lax.dot_general(
                    spread[v, :, hidden], tok[v], TN, preferred_element_type=jnp.float32
                )
            )
        for e in range(experts):
            total = acc[e, hidden]
            for v, term in zip(owners, terms):
                total = total + rv[v, e] * term
            acc[e, hidden] = total

    def receive(way, d, p):
        ag_copy(way, d, p, behind(way, d)).wait_recv()

    def forward(way, d, p):
        ag_copy(way, d + 1, p, behind(way, d)).start()

    def ag_step(d, owners, last):
        for p in range(4):
            for way in (0, 1):
                receive(way, d, p)
                if not last or p in start_pieces(half, way):
                    forward(way, d, p)
            back(owners, p)

    ag_step(1, (z,), False)
    lax.fori_loop(
        2,
        half - 1,
        lambda d, carry: (ag_step(d, (behind(0, d - 1), behind(1, d - 1)), False), carry)[1],
        0,
    )
    ag_step(half - 1, (behind(0, half - 2), behind(1, half - 2)), True)
    for i in range(4):
        back((behind(0, half - 1), behind(1, half - 1)), i)
    for way in (0, 1):
        for p in start_pieces(half, way):
            receive(way, half, p)
    for i in range(4):
        back((far,), i)
    wg[...] = acc[...].astype(jnp.bfloat16)

    for way in (0, 1):
        for p in range(4):
            reach = half if p in start_pieces(half, way) else half - 1

            def sent(d, carry, way=way, p=p):
                rs_copy(way, d, p, inbox.at[way, 0]).wait_send()
                ag_copy(way, d, p, 0).wait_send()
                return carry

            lax.fori_loop(1, reach + 1, sent, 0)


def ring(n, rv, wx, tok, ups):
    experts, hidden, depth = wx.shape
    rows = tok.shape[1]
    half = n // 2
    vmem = pl.BlockSpec(memory_space=pltpu.VMEM)
    return pl.pallas_call(
        functools.partial(ring_kernel, n),
        out_shape=(
            jax.ShapeDtypeStruct((n, rows, depth), jnp.bfloat16),
            jax.ShapeDtypeStruct((experts, hidden, depth), jnp.bfloat16),
        ),
        in_specs=[pl.BlockSpec(memory_space=pltpu.SMEM), vmem, vmem, vmem],
        out_specs=(vmem, vmem),
        scratch_shapes=[
            pltpu.VMEM((n, hidden, depth), jnp.bfloat16),
            pltpu.VMEM((2, rows, hidden), jnp.bfloat16),
            pltpu.VMEM((2, 2, rows, hidden), jnp.float32),
            pltpu.VMEM((2, half, rows, hidden), jnp.bfloat16),
            pltpu.VMEM((n, rows, hidden), jnp.bfloat16),
            pltpu.VMEM((experts, hidden, depth), jnp.float32),
            pltpu.SemaphoreType.DMA((2, half, 4)),
            pltpu.SemaphoreType.DMA((2, half, 4)),
            pltpu.SemaphoreType.DMA((2, half, 4)),
            pltpu.SemaphoreType.DMA((2, half, 4)),
        ],
        compiler_params=pltpu.CompilerParams(
            collective_id=0, has_side_effects=True, vmem_limit_bytes=48 * 2**20
        ),
    )(rv, wx, tok, ups)


def swap(a):
    return lax.ppermute(a, "core", [(0, 1), (1, 0)])


def exchange(a, axes):
    return lax.all_to_all(a, axes, split_axis=0, concat_axis=0, tiled=True)


def local(tokens, upstream, router, counts, w_gate, w_up):
    n = lax.axis_size("dp")
    z = lax.axis_index("dp")
    core = lax.axis_index("core")
    place = lax.axis_index(PLANE)
    _, slots, seg_len, width = tokens.shape
    _, depth, blocks, cols = w_gate.shape
    plane = lax.axis_size(PLANE)
    lines = seg_len // (2 * plane)
    first = core == 0

    empty, double = counts == 0, counts == 2
    before = jnp.tril(jnp.ones((n, n), jnp.int32), -1)
    empty_rank = jnp.sum(before * empty[None, :].astype(jnp.int32), 1)
    double_rank = jnp.sum(before * double[None, :].astype(jnp.int32), 1)
    pairs = (empty[:, None] & double[None, :]) & (empty_rank[:, None] == double_rank[None, :])
    ids = jnp.arange(n, dtype=jnp.int32)
    partner = jnp.sum(jnp.where(pairs, ids[None, :], 0), 1)
    helper = jnp.sum(jnp.where(pairs, ids[:, None], 0), 0)
    helped = jnp.sum(pairs.astype(jnp.int32), 0) > 0
    lent = jnp.sum(jnp.where(pairs[:, :, None], router[None, :, 1, :], 0.0), 1)
    rv = jnp.where(empty[:, None], lent, router[:, 0, :])

    own = jnp.concatenate([w_gate[0].transpose(1, 2, 0), w_up[0].transpose(1, 2, 0)], 1)
    own = exchange(own, EXPERT)
    other = swap(own)
    lo, hi = jnp.where(first, own, other), jnp.where(first, other, own)
    cut = 64
    wx = jnp.concatenate(
        [
            lo[:, :cols],
            hi[:, :cols],
            hi[:, 2 * cols - cut :],
            lo[:, cols:],
            hi[:, cols : 2 * cols - cut],
        ],
        1,
    )

    mine = lax.dynamic_slice_in_dim(tokens[0], (place * 2 + core) * lines, lines, 1)
    mine = exchange(mine.reshape(slots, lines, n, width // n).transpose(2, 0, 1, 3), "dp")
    mine = jnp.where(empty[:, None, None], jnp.take(mine[:, 1], partner, 0), mine[:, 0])
    tok = lax.all_gather(mine, PLANE).transpose(1, 0, 2, 3).reshape(n, plane * lines, -1)

    up = upstream[0].reshape(slots, plane, 2, lines, cols)
    own_up = jnp.where(first, up[:, :, 0], up[:, :, 1])
    other_up = swap(jnp.where(first, up[:, :, 1], up[:, :, 0]))
    up = jnp.concatenate(
        [jnp.where(first, own_up, other_up), jnp.where(first, other_up, own_up)], -1
    )
    moved = exchange(up[1], "dp")
    moved = exchange(jnp.take(moved, partner, 0), "dp")
    ups = jnp.where(counts[z] == 0, moved, up[0]).reshape(plane * lines, 2 * cols)
    ups = jnp.concatenate([ups, ups[:, 2 * cols - cut :]], 1)

    tg, wg = ring(n, rv, wx, tok, ups)

    tg = tg.reshape(n, plane, lines, -1).transpose(1, 0, 2, 3)
    tg = jnp.sum(exchange(tg, PLANE).reshape(plane, n, lines, -1).astype(jnp.float32), 0)
    tg = tg.astype(jnp.bfloat16)
    slot0 = jnp.where(empty[:, None, None], 0, tg)
    slot1 = jnp.where(helped[:, None, None], jnp.take(tg, helper, 0), 0)
    tg = exchange(jnp.stack([slot0, slot1], 1), "dp")
    tokens_grad = tg.transpose(1, 2, 0, 3).reshape(1, slots, lines, width)

    lo = jnp.concatenate([wg[:, :cols], wg[:, 2 * cols + cut : 3 * cols + cut]], 1)
    hi = jnp.concatenate(
        [wg[:, cols : 2 * cols], wg[:, 3 * cols + cut :], wg[:, 2 * cols : 2 * cols + cut]], 1
    )
    got = swap(jnp.where(first, hi, lo)).astype(jnp.float32)
    total = (jnp.where(first, lo, hi).astype(jnp.float32) + got).astype(jnp.bfloat16)
    total = exchange(total, EXPERT)
    gate_grad = total[:, :cols].transpose(2, 0, 1)[None]
    up_grad = total[:, cols:].transpose(2, 0, 1)[None]
    return (tokens_grad, gate_grad, up_grad)


def solution(mesh):
    shape = (mesh.shape["dp"], 2, mesh.shape["expert"] // 2, mesh.shape["tensor"] // 2, 2)
    fine = Mesh(mesh.devices.reshape(shape), ("dp", "y_lo", "x", "y_hi", "core"))
    tensor = ("y_hi", "core")
    weights = P(EXPERT, "dp", None, tensor)
    in_specs = (
        P("dp", None, None, None),
        P("dp", None, None, EXPERT + tensor),
        P(),
        P(),
        weights,
        weights,
    )
    out_specs = (P("dp", None, EXPERT + tensor, None), weights, weights)
    return jax.shard_map(local, mesh=fine, in_specs=in_specs, out_specs=out_specs, check_vma=False)
```

```python
import functools

import jax
import jax.numpy as jnp
from jax import lax
from jax.experimental import pallas as pl
from jax.experimental.pallas import tpu as pltpu
from jax.sharding import Mesh, PartitionSpec as P

MESH = pl.DeviceIdType.MESH
EXPERT = ("y_lo", "x")
PLANE = 16
ROWS = 176
TILES = 11
COLS = 224
PIECES = ((0, 48), (48, 48), (96, 48), (144, 32))
PARTS = ((0, 256), (256, 256), (512, 256), (768, 128))
NT = (((1,), (1,)), ((), ()))
TN = (((0,), (0,)), ((), ()))
f32, bf16 = jnp.float32, jnp.bfloat16


def loop(lo, hi, body):
    def step(i, carry):
        body(i)
        return carry

    lax.fori_loop(lo, hi, step, 0)


def kernel(
    n, counts, router, w_gate, w_up, tokens, upstream,
    out_tokens, out_gate, out_up,
    ids, rv, raw, zrecv, tokbuf, upsend, uprecv, upfull, up1, up2, upmoved,
    merged, stage, contrib, inbox, spread, acc,
    term, tg_out, tg_in, tg_send, tg_fin, sib_out, sib_in, wg_out,
    local_sem, w_send, w_recv, s_send, s_recv, tz_send, tz_recv, tp_send, tp_recv,
    us_sem, u1_send, u1_recv, u2_send, u2_recv,
    rs_send, rs_recv, ag_send, ag_recv,
    gp_send, gp_recv, gz_send, gz_recv, x_send, x_recv, e_send, e_recv,
):
    z = lax.axis_index("dp")
    y_lo, x, y_hi = lax.axis_index("y_lo"), lax.axis_index("x"), lax.axis_index("y_hi")
    core = lax.axis_index("core")
    expert = y_lo * 4 + x
    place = expert * 2 + y_hi
    half = n // 2
    experts = raw.shape[1]
    right, left = lax.rem(z + 1, n), lax.rem(z + n - 1, n)
    towards = (right, left)

    def on_plane(q, c):
        return {"y_lo": q // 8, "x": lax.rem(q // 2, 4), "y_hi": lax.rem(q, 2), "core": c}

    def on_expert(e):
        return {"y_lo": e // 4, "x": lax.rem(e, 4)}

    sibling = {"core": 1 - core}

    def remote(src, dst, send, recv, where):
        return pltpu.make_async_remote_copy(
            src_ref=src, dst_ref=dst, send_sem=send, recv_sem=recv,
            device_id=where, device_id_type=MESH,
        )

    def ahead(way, d):
        return lax.rem(z + d, n) if way == 0 else lax.rem(z + n - d, n)

    def behind(way, d):
        return ahead(1 - way, d)

    barrier = pltpu.get_barrier_semaphore()

    def greet(where):
        pl.semaphore_signal(barrier, inc=1, device_id=where, device_id_type=MESH)

    greet(sibling)
    loop(1, n, lambda k: greet({"dp": lax.rem(z + k, n)}))

    def greet_chip(k):
        q = lax.rem(place + k, PLANE)
        greet(on_plane(q, 0))
        greet(on_plane(q, 1))

    loop(1, PLANE, greet_chip)
    pl.semaphore_wait(barrier, 1 + (n - 1) + 2 * (PLANE - 1))

    tile = lax.rem(place + TILES * core, PLANE)
    serves = tile < TILES

    def token_block(to):
        rows = pl.ds(pl.multiple_of(core * ROWS + tile * 16, 16), 16)
        return tokens.at[:, rows, pl.ds(pl.multiple_of(to * 128, 128), 128)]

    def token_copy(k):
        to = lax.rem(z + k, n)
        return remote(token_block(to), zrecv.at[z], tz_send.at[k], tz_recv.at[k], {"dp": to})

    own_tokens = pltpu.make_async_copy(token_block(z), zrecv.at[z], local_sem.at[2])

    @pl.when(serves)
    def _():
        loop(1, n, lambda k: token_copy(k).start())
        own_tokens.start()

    stored = (w_gate, w_up)

    def weight_copy(k, w):
        to = lax.rem(expert + k, experts)
        return remote(
            stored[w].at[to], raw.at[core, expert, w], w_send.at[k, w], w_recv.at[k, w], on_expert(to)
        )

    def own_weights(w):
        return pltpu.make_async_copy(stored[w].at[expert], raw.at[core, expert, w], local_sem.at[w])

    for w in (0, 1):
        own_weights(w).start()

    def send_weights(k):
        for w in (0, 1):
            weight_copy(k, w).start()

    loop(1, experts, send_weights)

    row = lax.broadcasted_iota(jnp.int32, (ROWS, 2 * ROWS), 0)
    col = lax.broadcasted_iota(jnp.int32, (ROWS, 2 * ROWS), 1)
    unit = lax.broadcasted_iota(jnp.int32, (COLS, 512), 0)
    lane = lax.broadcasted_iota(jnp.int32, (COLS, 512), 1)
    tail = unit >= 192
    spot = jnp.where(
        tail, unit + (192 + 32 * core), (unit >> 6) * 128 + (unit & 63) + 64 * core
    )
    put = ((lane == spot) | (tail & (lane == spot + 64))).astype(f32).astype(bf16)

    def upstream_rows(k, which):
        pick = (col == row + ROWS * which).astype(f32).astype(bf16)
        turned = lax.dot_general(pick, upstream[k], NT, preferred_element_type=f32)
        return jnp.dot(turned.astype(bf16), put, preferred_element_type=f32).astype(bf16)

    for k in (0, 1):
        upsend[k] = upstream_rows(k, 1 - core)
    up_swap = remote(upsend, uprecv, us_sem.at[0], us_sem.at[1], sibling)
    up_swap.start()

    def ranks(g, carry):
        empties, doubles = carry
        ids[0, g] = empties
        ids[1, g] = doubles
        held = counts[g]
        return (
            empties + jnp.where(held == 0, 1, 0),
            doubles + jnp.where(held == 2, 1, 0),
        )

    lax.fori_loop(0, n, ranks, (jnp.int32(0), jnp.int32(0)))

    def pair(d):
        partner, helper = jnp.int32(0), jnp.int32(0)
        for g in range(n):
            lends = (counts[d] == 0) & (counts[g] == 2) & (ids[0, d] == ids[1, g])
            partner = partner + jnp.where(lends, g, 0)
            helps = (counts[g] == 0) & (counts[d] == 2) & (ids[0, g] == ids[1, d])
            helper = helper + jnp.where(helps, g, 0)
        ids[2, d] = partner
        ids[3, d] = helper
        source = jnp.where(counts[d] == 0, 2 * partner + 1, 2 * d)
        for e in range(experts):
            rv[d, e] = router[source, e]

    loop(0, n, pair)

    for k in (0, 1):
        upfull[k] = upstream_rows(k, core)

    def tile_copy(k):
        to = lax.rem(place + k, PLANE)
        return remote(
            tokbuf.at[tile], tokbuf.at[tile], tp_send.at[k], tp_recv.at[tile], on_plane(to, core)
        )

    @pl.when(serves)
    def _():
        loop(1, n, lambda k: token_copy(k).wait_recv())
        own_tokens.wait()

        def choose(v):
            lent, own = zrecv[ids[2, v], 1], zrecv[v, 0]
            tokbuf[tile, v] = jnp.where(counts[v] == 0, lent, own)

        loop(0, n, choose)
        loop(1, PLANE, lambda k: tile_copy(k).start())

    up_swap.wait()
    for k in (0, 1):
        upfull[k] = (upfull[k].astype(f32) + uprecv[k].astype(f32)).astype(bf16)

    def keeper(i):
        return lax.rem(i + half * core, n)

    kept = lax.rem(z + half * core, n)
    keeps = kept < TILES

    def scatter_copy(i):
        rows = pl.ds(pl.multiple_of(i * 16, 16), 16)
        return remote(
            upfull.at[1, rows], up1.at[z], u1_send.at[i], u1_recv.at[z], {"dp": keeper(i)}
        )

    def scatter(i):
        @pl.when(keeper(i) != z)
        def _():
            scatter_copy(i).start()

        @pl.when(keeper(i) == z)
        def _():
            up1[z] = upfull[1, pl.ds(pl.multiple_of(i * 16, 16), 16)]

    loop(0, TILES, scatter)

    def pass_block(e, w):
        return remote(
            raw.at[core, e, w], raw.at[core, e, w], s_send.at[e, w], s_recv.at[e, w], sibling
        )

    for w in (0, 1):
        own_weights(w).wait()
        pass_block(expert, w).start()

    def pass_weights(k):
        e = lax.rem(expert + experts - k, experts)
        for w in (0, 1):
            remote(
                stored[w].at[0], raw.at[core, e, w], w_send.at[k, w], w_recv.at[k, w], sibling
            ).wait_recv()
            pass_block(e, w).start()

    loop(1, experts, pass_weights)

    def await_weights(e):
        for w in (0, 1):
            remote(
                raw.at[core, e, w], raw.at[1 - core, e, w], s_send.at[e, w], s_recv.at[e, w], sibling
            ).wait_recv()

    loop(0, experts, await_weights)

    def await_tile(t):
        @pl.when(t != tile)
        def _():
            remote(
                tokbuf.at[t], tokbuf.at[t], tp_send.at[0], tp_recv.at[t], sibling
            ).wait_recv()

    loop(0, TILES, await_tile)

    def merge(v):
        weights = [rv[v, e] for e in range(experts)]

        def block(s, w, src, dst):
            total = weights[0] * raw[s, 0, w, src].astype(f32)
            for e in range(1, experts):
                total = total + weights[e] * raw[s, e, w, src].astype(f32)
            merged[v, dst] = total.astype(bf16)

        def tiles(q):
            for s in (0, 1):
                for w in (0, 1):
                    block(
                        s,
                        w,
                        pl.ds(pl.multiple_of(q * 64, 64), 64),
                        pl.ds(pl.multiple_of(w * 512 + q * 128 + s * 64, 64), 64),
                    )

        loop(0, 3, tiles)
        for s in (0, 1):
            for w in (0, 1):
                block(s, w, pl.ds(192, 32), pl.ds(384 + w * 64 + s * 32, 32))

    def tok(v):
        return tokbuf[:, v].reshape(ROWS, 128)

    def partial(v):
        return lax.dot_general(tok(v), merged[v], NT, preferred_element_type=f32)

    def rs_copy(way, d, p, src):
        rows = pl.ds(*PIECES[p])
        return remote(
            src.at[rows], inbox.at[way, d - 1, rows],
            rs_send.at[way, d - 1, p], rs_recv.at[way, d - 1, p], {"dp": towards[way]},
        )

    def ag_copy(way, d, p, v):
        rows = pl.ds(*PIECES[p])
        return remote(
            spread.at[v, rows], spread.at[v, rows],
            ag_send.at[way, d - 1, p], ag_recv.at[way, d - 1, p], {"dp": towards[way]},
        )

    def start_pieces(d, way):
        longer = (0, 1) if way == 0 else (2, 3)
        return longer if d == half else tuple(p for p in range(4) if p not in longer)

    far = ahead(0, half)
    merge(far)
    stage[0] = partial(far).astype(bf16)
    for way in (0, 1):
        for p in start_pieces(half, way):
            rs_copy(way, half, p, stage.at[0]).start()
    for way in (0, 1):
        v = ahead(way, half - 1)
        merge(v)
        contrib[(half - 1) % 2, way] = partial(v)
        for p in start_pieces(half - 1, way):
            rows = pl.ds(*PIECES[p])
            stage[1, rows] = contrib[(half - 1) % 2, way, rows].astype(bf16)
            rs_copy(way, half - 1, p, stage.at[1]).start()

    def gather_copy(k):
        to = lax.rem(z + k, n)
        rows = pl.ds(pl.multiple_of(kept * 16, 16), 16)
        return remote(up2.at[to], upmoved.at[rows], u2_send.at[k], u2_recv.at[kept], {"dp": to})

    @pl.when(keeps)
    def _():
        def await_scatter(k):
            g = lax.rem(z + k, n)
            remote(
                up2.at[0], up1.at[g], u1_send.at[0], u1_recv.at[g], {"dp": right}
            ).wait_recv()

        loop(1, n, await_scatter)

        def lend(d):
            up2[d] = up1[ids[2, d]]

        loop(0, n, lend)
        loop(1, n, lambda k: gather_copy(k).start())
        upmoved[pl.ds(pl.multiple_of(kept * 16, 16), 16)] = up2[z]

    def pass_on(way, d, p):
        rows = pl.ds(*PIECES[p])
        rs_copy(way, d + 1, p, inbox.at[way, d]).wait_recv()
        total = inbox[way, d, rows].astype(f32) + contrib[lax.rem(d, 2), way, rows]
        inbox[way, d, rows] = total.astype(bf16)
        rs_copy(way, d, p, inbox.at[way, d]).start()

    def prepare(d, i):
        way, second = i // 2, i % 2
        v = ahead(way, d)
        if second:
            contrib[lax.rem(d, 2), way] = partial(v)
        else:
            merge(v)

    for i in range(4):
        if i < 2:
            pass_on(0, half - 1, start_pieces(half, 0)[i])
            pass_on(1, half - 1, start_pieces(half, 1)[i])
        prepare(half - 2, i)

    def rs_step(i):
        d = half - 2 - i
        for j, (up, down) in enumerate(((2, 0), (3, 1), (0, 2), (1, 3))):
            pass_on(0, d, up)
            pass_on(1, d, down)
            prepare(d - 1, j)

    loop(0, half - 2, rs_step)

    def await_gather(i):
        @pl.when(i != kept)
        def _():
            rows = pl.ds(pl.multiple_of(i * 16, 16), 16)
            remote(
                up2.at[0], upmoved.at[rows], u2_send.at[0], u2_recv.at[i], {"dp": right}
            ).wait_recv()

    loop(0, TILES, await_gather)

    def gate_part(gate, up, flowing):
        s = jax.nn.sigmoid(gate)
        return (flowing * up * s * (1.0 + gate * (1.0 - s))).astype(bf16)

    def up_part(gate, flowing):
        return (flowing * gate * jax.nn.sigmoid(gate)).astype(bf16)

    for p in range(4):
        rows = pl.ds(*PIECES[p])
        for way in (0, 1):
            rs_copy(way, 1, p, inbox.at[way, 0]).wait_recv()
        pre = inbox[0, 0, rows].astype(f32) + inbox[1, 0, rows].astype(f32) + contrib[0, 0, rows]
        flowing = jnp.where(counts[z] == 0, upmoved[rows], upfull[0, rows]).astype(f32)
        gate, mixed, up = pre[:, :384], pre[:, 384:512], pre[:, 512:]
        spread[z, rows, :384] = gate_part(gate, up, flowing[:, :384])
        spread[z, rows, 512:] = up_part(gate, flowing[:, :384])
        low = lax.broadcasted_iota(jnp.int32, mixed.shape, 1) < 64
        rolled = pltpu.roll(mixed, 64, 1)
        gate, up = jnp.where(low, mixed, rolled), jnp.where(low, rolled, mixed)
        spread[z, rows, 384:512] = jnp.where(
            low, gate_part(gate, up, flowing[:, 384:]), up_part(gate, flowing[:, 384:])
        )
        for way in (0, 1):
            ag_copy(way, 1, p, z).start()

    acc[...] = jnp.zeros_like(acc)

    wide = lax.broadcasted_iota(jnp.int32, (PLANE * 16, ROWS), 0)
    slim = lax.broadcasted_iota(jnp.int32, (PLANE * 16, ROWS), 1)
    spare = (wide & 15) < TILES
    widen = (spare & (slim == (wide >> 4) * TILES + (wide & 15))).astype(f32).astype(bf16)
    my_block = x * 4 + y_hi * 2 + core

    def back(owners, i, unit):
        rows, hidden = pl.ds(*PIECES[i]), pl.ds(*PARTS[i])
        terms = []
        for j, v in enumerate(owners):
            term[j, rows] = jnp.dot(
                spread[v, rows], merged[v], preferred_element_type=f32
            ).astype(bf16)
            terms.append(
                lax.dot_general(spread[v, :, hidden], tok(v), TN, preferred_element_type=f32)
            )
            if i == 3:
                blocks = jnp.dot(widen, term[j], preferred_element_type=f32).astype(bf16)
                tg_out[:, unit + j] = blocks.reshape(PLANE, 16, 128)
        for e in range(experts):
            total = acc[e, hidden]
            for v, t in zip(owners, terms):
                total = total + rv[v, e] * t
            acc[e, hidden] = total
        if i == 3:
            send_terms(unit, len(owners))

    def term_copy(k, units):
        where = {"y_lo": core, "x": k // 4, "y_hi": lax.rem(k // 2, 2), "core": lax.rem(k, 2)}
        return remote(
            tg_out.at[k, units], tg_in.at[place, units], gp_send.at[k], gp_recv.at[place], where
        )

    def send_terms(unit, count):
        units = pl.ds(unit, count)

        def send(k):
            here = (y_lo == core) & (k == my_block)

            @pl.when(here)
            def _():
                tg_in[place, units] = tg_out[k, units]

            @pl.when(jnp.logical_not(here))
            def _():
                term_copy(k, units).start()

        loop(0, PLANE, send)

    def receive(way, d, p):
        ag_copy(way, d, p, behind(way, d)).wait_recv()

    def forward(way, d, p):
        ag_copy(way, d + 1, p, behind(way, d)).start()

    def ag_step(d, owners, last, unit):
        for p in range(4):
            for way in (0, 1):
                receive(way, d, p)
                if not last or p in start_pieces(half, way):
                    forward(way, d, p)
            back(owners, p, unit)

    ag_step(1, (z,), False, 0)
    loop(
        2,
        half - 1,
        lambda d: ag_step(d, (behind(0, d - 1), behind(1, d - 1)), False, 2 * d - 3),
    )
    ag_step(half - 1, (behind(0, half - 2), behind(1, half - 2)), True, n - 5)
    for i in range(4):
        back((behind(0, half - 1), behind(1, half - 1)), i, n - 3)
    for way in (0, 1):
        for p in start_pieces(half, way):
            receive(way, half, p)
    for i in range(4):
        back((far,), i, n - 1)

    other = 1 - core

    def units_of(w, s):
        for q in range(3):
            yield q * 64, 64, pl.ds(pl.multiple_of(w * 512 + q * 128 + s * 64, 64), 64)
        yield 192, 32, pl.ds(pl.multiple_of(384 + w * 64 + s * 32, 32), 32)

    def cross_copy(e):
        return remote(sib_out.at[e], sib_in.at[e], x_send.at[e], x_recv.at[e], sibling)

    def cross(e):
        for w in (0, 1):
            for at, size, hidden in units_of(w, other):
                sib_out[e, w, at : at + size] = acc[e, hidden].astype(bf16)
        cross_copy(e).start()

    loop(0, experts, cross)

    outs = (out_gate, out_up)

    def home_copy(k, w):
        to = lax.rem(expert + k, experts)
        return remote(
            wg_out.at[to, w], outs[w].at[expert], e_send.at[k, w], e_recv.at[k, w], on_expert(to)
        )

    def own_home(w):
        return pltpu.make_async_copy(wg_out.at[expert, w], outs[w].at[expert], local_sem.at[w])

    def settle(k):
        e = lax.rem(expert + k, experts)
        cross_copy(e).wait_recv()
        for w in (0, 1):
            for at, size, hidden in units_of(w, core):
                total = acc[e, hidden] + sib_in[e, w, at : at + size].astype(f32)
                wg_out[e, w, at : at + size] = total.astype(bf16)

        @pl.when(k < experts)
        def _():
            for w in (0, 1):
                home_copy(k, w).start()

    loop(1, experts + 1, settle)
    for w in (0, 1):
        own_home(w).start()

    def await_terms(q):
        @pl.when(jnp.logical_not((y_lo == core) & (q == place)))
        def _():
            remote(
                tg_in.at[q], tg_in.at[q], gp_send.at[0], gp_recv.at[q], sibling
            ).wait_recv()

    loop(0, PLANE, await_terms)
    sums = tg_in[0].astype(f32)
    for q in range(1, PLANE):
        sums = sums + tg_in[q].astype(f32)
    term_sum = tg_out.at[0]

    def await_sent(k):
        @pl.when(jnp.logical_not((y_lo == core) & (k == my_block)))
        def _():
            remote(
                tg_out.at[k], tg_in.at[0], gp_send.at[k], gp_recv.at[0], sibling
            ).wait_send()

    loop(0, PLANE, await_sent)
    term_sum[...] = sums.astype(bf16)

    def unit_of(v):
        apart = lax.rem(v - z + n, n)
        near = jnp.where(apart < half, 2 * apart, 2 * (n - apart) - 1)
        return jnp.where(apart == half, n - 1, near)

    def slots(g):
        nothing = jnp.zeros((16, 128), bf16)
        first, second = term_sum[unit_of(g)], term_sum[unit_of(ids[3, g])]
        tg_send[g, 0] = jnp.where(counts[g] == 0, nothing, first)
        tg_send[g, 1] = jnp.where(counts[g] == 2, second, nothing)

    loop(0, n, slots)

    def slot_copy(k):
        to = lax.rem(z + k, n)
        return remote(tg_send.at[to], tg_fin.at[z], gz_send.at[k], gz_recv.at[k], {"dp": to})

    loop(1, n, lambda k: slot_copy(k).start())
    tg_fin[z] = tg_send[z]

    for way in (0, 1):
        for p in range(4):
            reach = half if p in start_pieces(half, way) else half - 1

            def sent(d, way=way, p=p):
                rs_copy(way, d, p, inbox.at[way, 0]).wait_send()
                ag_copy(way, d, p, 0).wait_send()

            loop(1, reach + 1, sent)

    @pl.when(serves)
    def _():
        loop(1, n, lambda k: token_copy(k).wait_send())
        loop(1, PLANE, lambda k: tile_copy(k).wait_send())

    def weights_sent(k):
        for w in (0, 1):
            weight_copy(k, w).wait_send()

    loop(1, experts, weights_sent)

    def passed(e):
        for w in (0, 1):
            pass_block(e, w).wait_send()
        cross_copy(e).wait_send()

    loop(0, experts, passed)

    def scattered(i):
        @pl.when(keeper(i) != z)
        def _():
            scatter_copy(i).wait_send()

    loop(0, TILES, scattered)

    @pl.when(keeps)
    def _():
        loop(1, n, lambda k: gather_copy(k).wait_send())

    def home(k):
        for w in (0, 1):
            home_copy(k, w).wait()

    loop(1, experts, home)
    for w in (0, 1):
        own_home(w).wait()
    loop(1, n, lambda k: slot_copy(k).wait())
    out_tokens[...] = tg_fin[...]


def local(tokens, upstream, router, counts, w_gate, w_up):
    n = lax.axis_size("dp")
    _, slots, seg_len, width = tokens.shape
    _, depth, blocks, cols = w_gate.shape
    experts = router.shape[2]
    half = n // 2
    hidden = 4 * cols
    vmem, smem, hbm = (
        pl.BlockSpec(memory_space=space) for space in (pltpu.VMEM, pltpu.SMEM, pl.ANY)
    )
    dma = pltpu.SemaphoreType.DMA
    home = jax.ShapeDtypeStruct((blocks, cols, depth), bf16)
    tg, gate_grad, up_grad = pl.pallas_call(
        functools.partial(kernel, n),
        out_shape=(jax.ShapeDtypeStruct((n, slots, 16, depth), bf16), home, home),
        in_specs=[smem, smem, hbm, hbm, hbm, vmem],
        out_specs=(vmem, hbm, hbm),
        scratch_shapes=[
            pltpu.SMEM((4, n), jnp.int32),
            pltpu.SMEM((n, experts), f32),
            pltpu.VMEM((2, experts, 2, cols, depth), bf16),
            pltpu.VMEM((n, slots, 16, depth), bf16),
            pltpu.VMEM((TILES, n, 16, depth), bf16),
            pltpu.VMEM((slots, ROWS, 512), bf16),
            pltpu.VMEM((slots, ROWS, 512), bf16),
            pltpu.VMEM((slots, ROWS, 512), bf16),
            pltpu.VMEM((n, 16, 512), bf16),
            pltpu.VMEM((n, 16, 512), bf16),
            pltpu.VMEM((ROWS, 512), bf16),
            pltpu.VMEM((n, hidden, depth), bf16),
            pltpu.VMEM((2, ROWS, hidden), bf16),
            pltpu.VMEM((2, 2, ROWS, hidden), f32),
            pltpu.VMEM((2, half, ROWS, hidden), bf16),
            pltpu.VMEM((n, ROWS, hidden), bf16),
            pltpu.VMEM((experts, hidden, depth), f32),
            pltpu.VMEM((2, ROWS, depth), bf16),
            pltpu.VMEM((PLANE, n, 16, depth), bf16),
            pltpu.VMEM((PLANE, n, 16, depth), bf16),
            pltpu.VMEM((n, slots, 16, depth), bf16),
            pltpu.VMEM((n, slots, 16, depth), bf16),
            pltpu.VMEM((experts, 2, cols, depth), bf16),
            pltpu.VMEM((experts, 2, cols, depth), bf16),
            pltpu.VMEM((experts, 2, cols, depth), bf16),
            dma((3,)),
            dma((experts, 2)), dma((experts, 2)),
            dma((experts, 2)), dma((experts, 2)),
            dma((n,)), dma((n,)),
            dma((PLANE,)), dma((PLANE,)),
            dma((2,)),
            dma((TILES,)), dma((n,)),
            dma((n,)), dma((PLANE,)),
            dma((2, half, 4)), dma((2, half, 4)),
            dma((2, half, 4)), dma((2, half, 4)),
            dma((PLANE,)), dma((PLANE,)),
            dma((n,)), dma((n,)),
            dma((experts,)), dma((experts,)),
            dma((experts, 2)), dma((experts, 2)),
        ],
        compiler_params=pltpu.CompilerParams(
            collective_id=0, has_side_effects=True, vmem_limit_bytes=56 * 2**20
        ),
    )(
        counts,
        router.reshape(n * slots, experts),
        w_gate[0].transpose(1, 2, 0),
        w_up[0].transpose(1, 2, 0),
        tokens[0],
        upstream[0].transpose(0, 2, 1),
    )
    tokens_grad = tg[:, :, : seg_len // 32].transpose(1, 2, 0, 3).reshape(1, slots, -1, width)
    return (tokens_grad, gate_grad.transpose(2, 0, 1)[None], up_grad.transpose(2, 0, 1)[None])


def solution(mesh):
    shape = (mesh.shape["dp"], 2, mesh.shape["expert"] // 2, mesh.shape["tensor"] // 2, 2)
    fine = Mesh(mesh.devices.reshape(shape), ("dp", "y_lo", "x", "y_hi", "core"))
    tensor = ("y_hi", "core")
    weights = P(EXPERT, "dp", None, tensor)
    in_specs = (
        P("dp", None, None, None),
        P("dp", None, None, EXPERT + tensor),
        P(),
        P(),
        weights,
        weights,
    )
    out_specs = (P("dp", None, EXPERT + tensor, None), weights, weights)
    return jax.shard_map(local, mesh=fine, in_specs=in_specs, out_specs=out_specs, check_vma=False)
```

```python
import functools

import jax
import jax.numpy as jnp
from jax import lax
from jax.experimental import pallas as pl
from jax.experimental.pallas import tpu as pltpu
from jax.sharding import Mesh, PartitionSpec as P

MESH = pl.DeviceIdType.MESH
EXPERT = ("y_lo", "x")
PLANE = 16
ROWS = 176
TILES = 11
COLS = 224
PIECES = ((0, 48), (48, 48), (96, 48), (144, 32))
BATCHES = ((0, 3), (3, 13))
PARTS = ((0, 256), (256, 256), (512, 256), (768, 128))
NT = (((1,), (1,)), ((), ()))
TN = (((0,), (0,)), ((), ()))
f32, bf16 = jnp.float32, jnp.bfloat16


def loop(lo, hi, body):
    def step(i, carry):
        body(i)
        return carry

    lax.fori_loop(lo, hi, step, 0)


def kernel(
    n, counts, router, w_gate, w_up, tokens, upstream,
    out_tokens, out_gate, out_up,
    ids, rv, raw, zrecv, tokbuf, upsend, uprecv, upfull, up1, up2, upmoved,
    merged, contrib, inbox, spread, acc,
    term, tg_out, tg_in, tg_send, tg_fin, sib_out, sib_in, wg_out,
    local_sem, w_send, w_recv, s_send, s_recv, tz_send, tz_recv, tp_send, tp_recv,
    us_sem, u1_send, u1_recv, u2_send, u2_recv,
    rs_send, rs_recv, ag_send, ag_recv,
    gp_send, gp_recv, gz_send, gz_recv, x_send, x_recv, e_send, e_recv,
):
    z = lax.axis_index("dp")
    y_lo, x, y_hi = lax.axis_index("y_lo"), lax.axis_index("x"), lax.axis_index("y_hi")
    core = lax.axis_index("core")
    expert = y_lo * 4 + x
    place = expert * 2 + y_hi
    half = n // 2
    experts = raw.shape[1]
    right, left = lax.rem(z + 1, n), lax.rem(z + n - 1, n)
    towards = (right, left)

    def on_plane(q, c):
        return {"y_lo": q // 8, "x": lax.rem(q // 2, 4), "y_hi": lax.rem(q, 2), "core": c}

    def on_expert(e):
        return {"y_lo": e // 4, "x": lax.rem(e, 4)}

    sibling = {"core": 1 - core}

    def remote(src, dst, send, recv, where):
        return pltpu.make_async_remote_copy(
            src_ref=src, dst_ref=dst, send_sem=send, recv_sem=recv,
            device_id=where, device_id_type=MESH,
        )

    def ahead(way, d):
        return lax.rem(z + d, n) if way == 0 else lax.rem(z + n - d, n)

    def behind(way, d):
        return ahead(1 - way, d)

    barrier = pltpu.get_barrier_semaphore()

    def greet(where):
        pl.semaphore_signal(barrier, inc=1, device_id=where, device_id_type=MESH)

    greet(sibling)
    loop(1, n, lambda k: greet({"dp": lax.rem(z + k, n)}))

    def greet_chip(k):
        q = lax.rem(place + k, PLANE)
        greet(on_plane(q, 0))
        greet(on_plane(q, 1))

    loop(1, PLANE, greet_chip)
    pl.semaphore_wait(barrier, 1 + (n - 1) + 2 * (PLANE - 1))

    tile = lax.rem(place + TILES * core, PLANE)
    serves = tile < TILES

    def token_block(to):
        rows = pl.ds(pl.multiple_of(core * ROWS + tile * 16, 16), 16)
        return tokens.at[:, rows, pl.ds(pl.multiple_of(to * 128, 128), 128)]

    def token_copy(k):
        to = lax.rem(z + k, n)
        return remote(token_block(to), zrecv.at[z], tz_send.at[k], tz_recv.at[k], {"dp": to})

    own_tokens = pltpu.make_async_copy(token_block(z), zrecv.at[z], local_sem.at[2])

    @pl.when(serves)
    def _():
        loop(1, n, lambda k: token_copy(k).start())
        own_tokens.start()

    stored = (w_gate, w_up)

    def weight_copy(k, w):
        to = lax.rem(expert + k, experts)
        return remote(
            stored[w].at[to], raw.at[core, expert, w], w_send.at[k, w], w_recv.at[k, w], on_expert(to)
        )

    def own_weights(w):
        return pltpu.make_async_copy(stored[w].at[expert], raw.at[core, expert, w], local_sem.at[w])

    for w in (0, 1):
        own_weights(w).start()

    def send_weights(k):
        for w in (0, 1):
            weight_copy(k, w).start()

    loop(1, experts, send_weights)

    row = lax.broadcasted_iota(jnp.int32, (ROWS, 2 * ROWS), 0)
    col = lax.broadcasted_iota(jnp.int32, (ROWS, 2 * ROWS), 1)
    unit = lax.broadcasted_iota(jnp.int32, (COLS, 512), 0)
    lane = lax.broadcasted_iota(jnp.int32, (COLS, 512), 1)
    tail = unit >= 192
    spot = jnp.where(
        tail, unit + (192 + 32 * core), (unit >> 6) * 128 + (unit & 63) + 64 * core
    )
    put = ((lane == spot) | (tail & (lane == spot + 64))).astype(f32).astype(bf16)

    def upstream_rows(k, which):
        pick = (col == row + ROWS * which).astype(f32).astype(bf16)
        turned = lax.dot_general(pick, upstream[k], NT, preferred_element_type=f32)
        return jnp.dot(turned.astype(bf16), put, preferred_element_type=f32).astype(bf16)

    for k in (0, 1):
        upsend[k] = upstream_rows(k, 1 - core)
    up_swap = remote(upsend, uprecv, us_sem.at[0], us_sem.at[1], sibling)
    up_swap.start()

    def ranks(g, carry):
        empties, doubles = carry
        ids[0, g] = empties
        ids[1, g] = doubles
        held = counts[g]
        return (
            empties + jnp.where(held == 0, 1, 0),
            doubles + jnp.where(held == 2, 1, 0),
        )

    lax.fori_loop(0, n, ranks, (jnp.int32(0), jnp.int32(0)))

    def pair(d):
        partner, helper = jnp.int32(0), jnp.int32(0)
        for g in range(n):
            lends = (counts[d] == 0) & (counts[g] == 2) & (ids[0, d] == ids[1, g])
            partner = partner + jnp.where(lends, g, 0)
            helps = (counts[g] == 0) & (counts[d] == 2) & (ids[0, g] == ids[1, d])
            helper = helper + jnp.where(helps, g, 0)
        ids[2, d] = partner
        ids[3, d] = helper
        slot = jnp.where(counts[d] == 0, 1, 0)
        group = jnp.where(counts[d] == 0, partner, d)
        for e in range(experts):
            rv[d, e] = router[slot, e, group]

    loop(0, n, pair)

    for k in (0, 1):
        upfull[k] = upstream_rows(k, core)

    up_swap.wait()
    for k in (0, 1):
        upfull[k] = (upfull[k].astype(f32) + uprecv[k].astype(f32)).astype(bf16)

    def keeper(i):
        return lax.rem(i + half * core, n)

    kept = lax.rem(z + half * core, n)
    keeps = kept < TILES

    def scatter_copy(i):
        rows = pl.ds(pl.multiple_of(i * 16, 16), 16)
        return remote(
            upfull.at[1, rows], up1.at[z], u1_send.at[i], u1_recv.at[z], {"dp": keeper(i)}
        )

    def scatter(i):
        @pl.when(keeper(i) != z)
        def _():
            scatter_copy(i).start()

        @pl.when(keeper(i) == z)
        def _():
            up1[z] = upfull[1, pl.ds(pl.multiple_of(i * 16, 16), 16)]

    loop(0, TILES, scatter)

    def order(v):
        return lax.rem(v - z + half + 1 + n, n)

    def tile_copy(k, b):
        to = lax.rem(place + k, PLANE)
        some = pl.ds(*BATCHES[b])
        return remote(
            tokbuf.at[tile, some], tokbuf.at[tile, some],
            tp_send.at[b, k], tp_recv.at[b, tile], on_plane(to, core),
        )

    @pl.when(serves)
    def _():
        loop(1, n, lambda k: token_copy(k).wait_recv())
        own_tokens.wait()

        def choose(v):
            lent, own = zrecv[ids[2, v], 1], zrecv[v, 0]
            tokbuf[tile, order(v)] = jnp.where(counts[v] == 0, lent, own)

        loop(0, n, choose)
        for b in (0, 1):
            loop(1, PLANE, lambda k, b=b: tile_copy(k, b).start())

    def pass_block(e, w):
        return remote(
            raw.at[core, e, w], raw.at[core, e, w], s_send.at[e, w], s_recv.at[e, w], sibling
        )

    for w in (0, 1):
        own_weights(w).wait()
        pass_block(expert, w).start()

    def pass_weights(k):
        e = lax.rem(expert + experts - k, experts)
        for w in (0, 1):
            remote(
                stored[w].at[0], raw.at[core, e, w], w_send.at[k, w], w_recv.at[k, w], sibling
            ).wait_recv()
            pass_block(e, w).start()

    loop(1, experts, pass_weights)

    def gather_copy(k):
        to = lax.rem(z + k, n)
        rows = pl.ds(pl.multiple_of(kept * 16, 16), 16)
        return remote(up2.at[to], upmoved.at[rows], u2_send.at[k], u2_recv.at[kept], {"dp": to})

    @pl.when(keeps)
    def _():
        def await_scatter(k):
            g = lax.rem(z + k, n)
            remote(
                up2.at[0], up1.at[g], u1_send.at[0], u1_recv.at[g], {"dp": right}
            ).wait_recv()

        loop(1, n, await_scatter)

        def lend(d):
            up2[d] = up1[ids[2, d]]

        loop(0, n, lend)
        loop(1, n, lambda k: gather_copy(k).start())
        upmoved[pl.ds(pl.multiple_of(kept * 16, 16), 16)] = up2[z]

    def await_weights(e):
        for w in (0, 1):
            remote(
                raw.at[core, e, w], raw.at[1 - core, e, w], s_send.at[e, w], s_recv.at[e, w], sibling
            ).wait_recv()

    loop(0, experts, await_weights)

    def await_tiles(b):
        some = pl.ds(*BATCHES[b])

        def await_tile(t):
            @pl.when(t != tile)
            def _():
                remote(
                    tokbuf.at[t, some], tokbuf.at[t, some], tp_send.at[b, 0], tp_recv.at[b, t], sibling
                ).wait_recv()

        loop(0, TILES, await_tile)

    await_tiles(0)

    def merge(v):
        weights = [rv[v, e] for e in range(experts)]

        def block(s, w, src, dst):
            total = weights[0] * raw[s, 0, w, src].astype(f32)
            for e in range(1, experts):
                total = total + weights[e] * raw[s, e, w, src].astype(f32)
            merged[v, dst] = total.astype(bf16)

        def tiles(q):
            for s in (0, 1):
                for w in (0, 1):
                    block(
                        s,
                        w,
                        pl.ds(pl.multiple_of(q * 64, 64), 64),
                        pl.ds(pl.multiple_of(w * 512 + q * 128 + s * 64, 64), 64),
                    )

        loop(0, 3, tiles)
        for s in (0, 1):
            for w in (0, 1):
                block(s, w, pl.ds(192, 32), pl.ds(384 + w * 64 + s * 32, 32))

    def tok(v):
        return tokbuf[:, order(v)].reshape(ROWS, 128)

    def partial(v):
        return lax.dot_general(tok(v), merged[v], NT, preferred_element_type=f32)

    def rs_copy(way, d, p):
        rows = pl.ds(*PIECES[p])
        return remote(
            inbox.at[way, d, rows], inbox.at[way, d - 1, rows],
            rs_send.at[way, p], rs_recv.at[way, d - 1, p], {"dp": towards[way]},
        )

    def ag_copy(way, d, p, v):
        rows = pl.ds(*PIECES[p])
        return remote(
            spread.at[v, rows], spread.at[v, rows],
            ag_send.at[way, d - 1, p], ag_recv.at[way, d - 1, p], {"dp": towards[way]},
        )

    def start_pieces(d, way):
        longer = (0, 1) if way == 0 else (2, 3)
        return longer if d == half else tuple(p for p in range(4) if p not in longer)

    far = ahead(0, half)
    merge(far)
    first = partial(far).astype(bf16)
    for way in (0, 1):
        for p in start_pieces(half, way):
            at, size = PIECES[p]
            inbox[way, half, at : at + size] = first[at : at + size]
            rs_copy(way, half, p).start()
    for way in (0, 1):
        v = ahead(way, half - 1)
        merge(v)
        contrib[(half - 1) % 2, way] = partial(v)
        for p in start_pieces(half - 1, way):
            rows = pl.ds(*PIECES[p])
            inbox[way, half - 1, rows] = contrib[(half - 1) % 2, way, rows].astype(bf16)
            rs_copy(way, half - 1, p).start()
    await_tiles(1)

    def pass_on(way, d, p):
        rows = pl.ds(*PIECES[p])
        rs_copy(way, d + 1, p).wait_recv()
        total = inbox[way, d, rows].astype(f32) + contrib[lax.rem(d, 2), way, rows]
        inbox[way, d, rows] = total.astype(bf16)
        rs_copy(way, d, p).start()

    def prepare(d, i):
        way, second = i // 2, i % 2
        v = ahead(way, d)
        if second:
            contrib[lax.rem(d, 2), way] = partial(v)
        else:
            merge(v)

    for i in range(4):
        if i < 2:
            pass_on(0, half - 1, start_pieces(half, 0)[i])
            pass_on(1, half - 1, start_pieces(half, 1)[i])
        prepare(half - 2, i)

    def rs_step(i):
        d = half - 2 - i
        for j, (up, down) in enumerate(((2, 0), (3, 1), (0, 2), (1, 3))):
            pass_on(0, d, up)
            pass_on(1, d, down)
            prepare(d - 1, j)

    loop(0, half - 2, rs_step)

    def await_gather(i):
        @pl.when(i != kept)
        def _():
            rows = pl.ds(pl.multiple_of(i * 16, 16), 16)
            remote(
                up2.at[0], upmoved.at[rows], u2_send.at[0], u2_recv.at[i], {"dp": right}
            ).wait_recv()

    loop(0, TILES, await_gather)

    def gate_part(gate, up, flowing):
        s = jax.nn.sigmoid(gate)
        return (flowing * up * s * (1.0 + gate * (1.0 - s))).astype(bf16)

    def up_part(gate, flowing):
        return (flowing * gate * jax.nn.sigmoid(gate)).astype(bf16)

    for p in range(4):
        rows = pl.ds(*PIECES[p])
        for way in (0, 1):
            rs_copy(way, 1, p).wait_recv()
        pre = inbox[0, 0, rows].astype(f32) + inbox[1, 0, rows].astype(f32) + contrib[0, 0, rows]
        flowing = jnp.where(counts[z] == 0, upmoved[rows], upfull[0, rows]).astype(f32)
        gate, mixed, up = pre[:, :384], pre[:, 384:512], pre[:, 512:]
        spread[z, rows, :384] = gate_part(gate, up, flowing[:, :384])
        spread[z, rows, 512:] = up_part(gate, flowing[:, :384])
        low = lax.broadcasted_iota(jnp.int32, mixed.shape, 1) < 64
        rolled = pltpu.roll(mixed, 64, 1)
        gate, up = jnp.where(low, mixed, rolled), jnp.where(low, rolled, mixed)
        spread[z, rows, 384:512] = jnp.where(
            low, gate_part(gate, up, flowing[:, 384:]), up_part(gate, flowing[:, 384:])
        )
        for way in (0, 1):
            ag_copy(way, 1, p, z).start()

    acc[...] = jnp.zeros_like(acc)

    wide = lax.broadcasted_iota(jnp.int32, (PLANE * 16, ROWS), 0)
    slim = lax.broadcasted_iota(jnp.int32, (PLANE * 16, ROWS), 1)
    spare = (wide & 15) < TILES
    widen = (spare & (slim == (wide >> 4) * TILES + (wide & 15))).astype(f32).astype(bf16)
    my_block = x * 4 + y_hi * 2 + core

    def back(owners, i, unit):
        rows, hidden = pl.ds(*PIECES[i]), pl.ds(*PARTS[i])
        terms = []
        for j, v in enumerate(owners):
            term[j, rows] = jnp.dot(
                spread[v, rows], merged[v], preferred_element_type=f32
            ).astype(bf16)
            terms.append(
                lax.dot_general(spread[v, :, hidden], tok(v), TN, preferred_element_type=f32)
            )
            if i == 3:
                blocks = jnp.dot(widen, term[j], preferred_element_type=f32).astype(bf16)
                tg_out[:, unit + j] = blocks.reshape(PLANE, 16, 128)
        for e in range(experts):
            total = acc[e, hidden]
            for v, t in zip(owners, terms):
                total = total + rv[v, e] * t
            acc[e, hidden] = total
        if i == 3:
            send_terms(unit, len(owners))

    def term_copy(k, units):
        where = {"y_lo": core, "x": k // 4, "y_hi": lax.rem(k // 2, 2), "core": lax.rem(k, 2)}
        return remote(
            tg_out.at[k, units], tg_in.at[place, units], gp_send.at[k], gp_recv.at[place], where
        )

    def send_terms(unit, count):
        units = pl.ds(unit, count)

        def send(k):
            here = (y_lo == core) & (k == my_block)

            @pl.when(here)
            def _():
                tg_in[place, units] = tg_out[k, units]

            @pl.when(jnp.logical_not(here))
            def _():
                term_copy(k, units).start()

        loop(0, PLANE, send)

    def receive(way, d, p):
        ag_copy(way, d, p, behind(way, d)).wait_recv()

    def forward(way, d, p):
        ag_copy(way, d + 1, p, behind(way, d)).start()

    def ag_step(d, owners, last, unit):
        for p in range(4):
            for way in (0, 1):
                receive(way, d, p)
                if not last or p in start_pieces(half, way):
                    forward(way, d, p)
            back(owners, p, unit)

    ag_step(1, (z,), False, 0)
    loop(
        2,
        half - 1,
        lambda d: ag_step(d, (behind(0, d - 1), behind(1, d - 1)), False, 2 * d - 3),
    )
    ag_step(half - 1, (behind(0, half - 2), behind(1, half - 2)), True, n - 5)
    for i in range(4):
        back((behind(0, half - 1), behind(1, half - 1)), i, n - 3)
    for way in (0, 1):
        for p in start_pieces(half, way):
            receive(way, half, p)
    for i in range(4):
        back((far,), i, n - 1)

    other = 1 - core

    def units_of(w, s):
        for q in range(3):
            yield q * 64, 64, pl.ds(pl.multiple_of(w * 512 + q * 128 + s * 64, 64), 64)
        yield 192, 32, pl.ds(pl.multiple_of(384 + w * 64 + s * 32, 32), 32)

    def cross_copy(e):
        return remote(sib_out.at[e], sib_in.at[e], x_send.at[e], x_recv.at[e], sibling)

    def cross(e):
        for w in (0, 1):
            for at, size, hidden in units_of(w, other):
                sib_out[e, w, at : at + size] = acc[e, hidden].astype(bf16)
        cross_copy(e).start()

    loop(0, experts, cross)

    outs = (out_gate, out_up)

    def home_copy(k, w):
        to = lax.rem(expert + k, experts)
        return remote(
            wg_out.at[to, w], outs[w].at[expert], e_send.at[k, w], e_recv.at[k, w], on_expert(to)
        )

    def own_home(w):
        return pltpu.make_async_copy(wg_out.at[expert, w], outs[w].at[expert], local_sem.at[w])

    def settle(k):
        e = lax.rem(expert + k, experts)
        cross_copy(e).wait_recv()
        for w in (0, 1):
            for at, size, hidden in units_of(w, core):
                total = acc[e, hidden] + sib_in[e, w, at : at + size].astype(f32)
                wg_out[e, w, at : at + size] = total.astype(bf16)

        @pl.when(k < experts)
        def _():
            for w in (0, 1):
                home_copy(k, w).start()

    loop(1, experts + 1, settle)
    for w in (0, 1):
        own_home(w).start()

    def await_terms(q):
        @pl.when(jnp.logical_not((y_lo == core) & (q == place)))
        def _():
            remote(
                tg_in.at[q], tg_in.at[q], gp_send.at[0], gp_recv.at[q], sibling
            ).wait_recv()

    loop(0, PLANE, await_terms)
    sums = tg_in[0].astype(f32)
    for q in range(1, PLANE):
        sums = sums + tg_in[q].astype(f32)
    term_sum = tg_out.at[0]

    def await_sent(k):
        @pl.when(jnp.logical_not((y_lo == core) & (k == my_block)))
        def _():
            remote(
                tg_out.at[k], tg_in.at[0], gp_send.at[k], gp_recv.at[0], sibling
            ).wait_send()

    loop(0, PLANE, await_sent)
    term_sum[...] = sums.astype(bf16)

    def unit_of(v):
        apart = lax.rem(v - z + n, n)
        near = jnp.where(apart < half, 2 * apart, 2 * (n - apart) - 1)
        return jnp.where(apart == half, n - 1, near)

    def slots(g):
        nothing = jnp.zeros((16, 128), bf16)
        first, second = term_sum[unit_of(g)], term_sum[unit_of(ids[3, g])]
        tg_send[g, 0] = jnp.where(counts[g] == 0, nothing, first)
        tg_send[g, 1] = jnp.where(counts[g] == 2, second, nothing)

    loop(0, n, slots)

    def slot_copy(k):
        to = lax.rem(z + k, n)
        return remote(tg_send.at[to], tg_fin.at[z], gz_send.at[k], gz_recv.at[k], {"dp": to})

    loop(1, n, lambda k: slot_copy(k).start())
    tg_fin[z] = tg_send[z]

    for way in (0, 1):
        for p in range(4):
            reach = half if p in start_pieces(half, way) else half - 1

            def sent(d, way=way, p=p):
                ag_copy(way, d, p, 0).wait_send()

            loop(1, reach + 1, sent)
            started = inbox.at[way, pl.ds(1, reach), pl.ds(*PIECES[p])]
            remote(
                started, started, rs_send.at[way, p], rs_recv.at[way, 0, p], sibling
            ).wait_send()

    @pl.when(serves)
    def _():
        loop(1, n, lambda k: token_copy(k).wait_send())
        for b in (0, 1):
            loop(1, PLANE, lambda k, b=b: tile_copy(k, b).wait_send())

    def weights_sent(k):
        for w in (0, 1):
            weight_copy(k, w).wait_send()

    loop(1, experts, weights_sent)

    def passed(e):
        for w in (0, 1):
            pass_block(e, w).wait_send()
        cross_copy(e).wait_send()

    loop(0, experts, passed)

    def scattered(i):
        @pl.when(keeper(i) != z)
        def _():
            scatter_copy(i).wait_send()

    loop(0, TILES, scattered)

    @pl.when(keeps)
    def _():
        loop(1, n, lambda k: gather_copy(k).wait_send())

    def home(k):
        for w in (0, 1):
            home_copy(k, w).wait()

    loop(1, experts, home)
    for w in (0, 1):
        own_home(w).wait()
    loop(1, n, lambda k: slot_copy(k).wait())
    out_tokens[...] = tg_fin[...]


def finish_kernel(gate, up, out_gate, out_up, sems):
    pieces = sems.shape[1]
    size = gate.shape[0] // pieces
    for go in (True, False):
        for w, (src, dst) in enumerate(((gate, out_gate), (up, out_up))):
            for i in range(pieces):
                some = pl.ds(i * size, size)
                copy = pltpu.make_async_copy(src.at[some], dst.at[some], sems.at[w, i])
                copy.start() if go else copy.wait()


def local(tokens, upstream, router, counts, w_gate, w_up):
    n = lax.axis_size("dp")
    _, slots, seg_len, width = tokens.shape
    _, depth, blocks, cols = w_gate.shape
    experts = router.shape[2]
    half = n // 2
    hidden = 4 * cols
    vmem, smem, hbm = (
        pl.BlockSpec(memory_space=space) for space in (pltpu.VMEM, pltpu.SMEM, pl.ANY)
    )
    dma = pltpu.SemaphoreType.DMA
    home = jax.ShapeDtypeStruct((blocks, cols, depth), bf16)
    tg, gate_grad, up_grad = pl.pallas_call(
        functools.partial(kernel, n),
        out_shape=(jax.ShapeDtypeStruct((n, slots, 16, depth), bf16), home, home),
        in_specs=[smem, smem, hbm, hbm, hbm, vmem],
        out_specs=(vmem, hbm, hbm),
        scratch_shapes=[
            pltpu.SMEM((4, n), jnp.int32),
            pltpu.SMEM((n, experts), f32),
            pltpu.VMEM((2, experts, 2, cols, depth), bf16),
            pltpu.VMEM((n, slots, 16, depth), bf16),
            pltpu.VMEM((TILES, n, 16, depth), bf16),
            pltpu.VMEM((slots, ROWS, 512), bf16),
            pltpu.VMEM((slots, ROWS, 512), bf16),
            pltpu.VMEM((slots, ROWS, 512), bf16),
            pltpu.VMEM((n, 16, 512), bf16),
            pltpu.VMEM((n, 16, 512), bf16),
            pltpu.VMEM((ROWS, 512), bf16),
            pltpu.VMEM((n, hidden, depth), bf16),
            pltpu.VMEM((2, 2, ROWS, hidden), f32),
            pltpu.VMEM((2, half + 1, ROWS, hidden), bf16),
            pltpu.VMEM((n, ROWS, hidden), bf16),
            pltpu.VMEM((experts, hidden, depth), f32),
            pltpu.VMEM((2, ROWS, depth), bf16),
            pltpu.VMEM((PLANE, n, 16, depth), bf16),
            pltpu.VMEM((PLANE, n, 16, depth), bf16),
            pltpu.VMEM((n, slots, 16, depth), bf16),
            pltpu.VMEM((n, slots, 16, depth), bf16),
            pltpu.VMEM((experts, 2, cols, depth), bf16),
            pltpu.VMEM((experts, 2, cols, depth), bf16),
            pltpu.VMEM((experts, 2, cols, depth), bf16),
            dma((3,)),
            dma((experts, 2)), dma((experts, 2)),
            dma((experts, 2)), dma((experts, 2)),
            dma((n,)), dma((n,)),
            dma((2, PLANE)), dma((2, TILES)),
            dma((2,)),
            dma((TILES,)), dma((n,)),
            dma((n,)), dma((PLANE,)),
            dma((2, 4)), dma((2, half, 4)),
            dma((2, half, 4)), dma((2, half, 4)),
            dma((PLANE,)), dma((PLANE,)),
            dma((n,)), dma((n,)),
            dma((experts,)), dma((experts,)),
            dma((experts, 2)), dma((experts, 2)),
        ],
        compiler_params=pltpu.CompilerParams(
            collective_id=0, has_side_effects=True, vmem_limit_bytes=56 * 2**20
        ),
    )(
        counts,
        router.transpose(1, 2, 0),
        w_gate[0].transpose(1, 2, 0),
        w_up[0].transpose(1, 2, 0),
        tokens[0],
        upstream[0].transpose(0, 2, 1),
    )
    gate_grad, up_grad = pl.pallas_call(
        finish_kernel,
        out_shape=(home, home),
        in_specs=[vmem, vmem],
        out_specs=(hbm, hbm),
        scratch_shapes=[dma((2, 4))],
    )(gate_grad, up_grad)
    tokens_grad = tg[:, :, : seg_len // 32].transpose(1, 2, 0, 3).reshape(1, slots, -1, width)
    return (tokens_grad, gate_grad.transpose(2, 0, 1)[None], up_grad.transpose(2, 0, 1)[None])


def solution(mesh):
    shape = (mesh.shape["dp"], 2, mesh.shape["expert"] // 2, mesh.shape["tensor"] // 2, 2)
    fine = Mesh(mesh.devices.reshape(shape), ("dp", "y_lo", "x", "y_hi", "core"))
    tensor = ("y_hi", "core")
    weights = P(EXPERT, "dp", None, tensor)
    in_specs = (
        P("dp", None, None, None),
        P("dp", None, None, EXPERT + tensor),
        P(),
        P(),
        weights,
        weights,
    )
    out_specs = (P("dp", None, EXPERT + tensor, None), weights, weights)
    return jax.shard_map(local, mesh=fine, in_specs=in_specs, out_specs=out_specs, check_vma=False)
```

```python
import functools

import jax
import jax.numpy as jnp
from jax import lax
from jax.experimental import pallas as pl
from jax.experimental.pallas import tpu as pltpu
from jax.sharding import Mesh, PartitionSpec as P

MESH = pl.DeviceIdType.MESH
EXPERT = ("y_lo", "x")
PLANE = 16
ROWS = 176
TILES = 11
COLS = 224
PIECES = ((0, 48), (48, 48), (96, 48), (144, 32))
BATCHES = ((0, 3), (3, 13))
PARTS = ((0, 256), (256, 256), (512, 256), (768, 128))
NT = (((1,), (1,)), ((), ()))
TN = (((0,), (0,)), ((), ()))
f32, bf16 = jnp.float32, jnp.bfloat16


def loop(lo, hi, body):
    def step(i, carry):
        body(i)
        return carry

    lax.fori_loop(lo, hi, step, 0)


def kernel(
    n, counts, router, w_gate, w_up, tokens, upstream,
    out_tokens, out_gate, out_up,
    ids, rv, raw, zrecv, tokbuf, upsend, uprecv, upfull, up1, up2, upmoved,
    merged, contrib, inbox, spread, acc,
    term, tg_out, tg_in, tg_send, tg_fin, sib_out, sib_in, wg_out,
    local_sem, w_send, w_recv, s_send, s_recv, tz_send, tz_recv, tp_send, tp_recv,
    us_sem, u1_send, u1_recv, u2_send, u2_recv,
    rs_send, rs_recv, ag_send, ag_recv,
    gp_send, gp_recv, gz_send, gz_recv, x_send, x_recv, e_send, e_recv,
):
    z = lax.axis_index("dp")
    y_lo, x, y_hi = lax.axis_index("y_lo"), lax.axis_index("x"), lax.axis_index("y_hi")
    core = lax.axis_index("core")
    expert = y_lo * 4 + x
    place = expert * 2 + y_hi
    half = n // 2
    experts = raw.shape[1]
    right, left = lax.rem(z + 1, n), lax.rem(z + n - 1, n)
    towards = (right, left)

    def on_plane(q, c):
        return {"y_lo": q // 8, "x": lax.rem(q // 2, 4), "y_hi": lax.rem(q, 2), "core": c}

    def on_expert(e):
        return {"y_lo": e // 4, "x": lax.rem(e, 4)}

    sibling = {"core": 1 - core}

    def remote(src, dst, send, recv, where):
        return pltpu.make_async_remote_copy(
            src_ref=src, dst_ref=dst, send_sem=send, recv_sem=recv,
            device_id=where, device_id_type=MESH,
        )

    def ahead(way, d):
        return lax.rem(z + d, n) if way == 0 else lax.rem(z + n - d, n)

    def behind(way, d):
        return ahead(1 - way, d)

    barrier = pltpu.get_barrier_semaphore()

    def greet(where):
        pl.semaphore_signal(barrier, inc=1, device_id=where, device_id_type=MESH)

    greet(sibling)
    loop(1, n, lambda k: greet({"dp": lax.rem(z + k, n)}))

    def greet_chip(k):
        q = lax.rem(place + k, PLANE)
        greet(on_plane(q, 0))
        greet(on_plane(q, 1))

    loop(1, PLANE, greet_chip)
    pl.semaphore_wait(barrier, 1 + (n - 1) + 2 * (PLANE - 1))

    tile = lax.rem(place + TILES * core, PLANE)
    serves = tile < TILES

    def token_block(to):
        rows = pl.ds(pl.multiple_of(core * ROWS + tile * 16, 16), 16)
        return tokens.at[:, rows, pl.ds(pl.multiple_of(to * 128, 128), 128)]

    def token_copy(k):
        to = lax.rem(z + k, n)
        return remote(token_block(to), zrecv.at[z], tz_send.at[k], tz_recv.at[k], {"dp": to})

    own_tokens = pltpu.make_async_copy(token_block(z), zrecv.at[z], local_sem.at[2])

    @pl.when(serves)
    def _():
        loop(1, n, lambda k: token_copy(k).start())
        own_tokens.start()

    stored = (w_gate, w_up)

    def weight_copy(k, w):
        to = lax.rem(expert + k, experts)
        return remote(
            stored[w].at[to], raw.at[core, expert, w], w_send.at[k, w], w_recv.at[k, w], on_expert(to)
        )

    def own_weights(w):
        return pltpu.make_async_copy(stored[w].at[expert], raw.at[core, expert, w], local_sem.at[w])

    for w in (0, 1):
        own_weights(w).start()

    def send_weights(k):
        for w in (0, 1):
            weight_copy(k, w).start()

    loop(1, experts, send_weights)

    row = lax.broadcasted_iota(jnp.int32, (ROWS, 2 * ROWS), 0)
    col = lax.broadcasted_iota(jnp.int32, (ROWS, 2 * ROWS), 1)
    unit = lax.broadcasted_iota(jnp.int32, (COLS, 512), 0)
    lane = lax.broadcasted_iota(jnp.int32, (COLS, 512), 1)
    tail = unit >= 192
    spot = jnp.where(
        tail, unit + (192 + 32 * core), (unit >> 6) * 128 + (unit & 63) + 64 * core
    )
    put = ((lane == spot) | (tail & (lane == spot + 64))).astype(f32).astype(bf16)

    def upstream_rows(k, which):
        pick = (col == row + ROWS * which).astype(f32).astype(bf16)
        turned = lax.dot_general(pick, upstream[k], NT, preferred_element_type=f32)
        return jnp.dot(turned.astype(bf16), put, preferred_element_type=f32).astype(bf16)

    for k in (0, 1):
        upsend[k] = upstream_rows(k, 1 - core)
    up_swap = remote(upsend, uprecv, us_sem.at[0], us_sem.at[1], sibling)
    up_swap.start()

    def ranks(g, carry):
        empties, doubles = carry
        ids[0, g] = empties
        ids[1, g] = doubles
        held = counts[g]
        return (
            empties + jnp.where(held == 0, 1, 0),
            doubles + jnp.where(held == 2, 1, 0),
        )

    lax.fori_loop(0, n, ranks, (jnp.int32(0), jnp.int32(0)))

    def pair(d):
        partner, helper = jnp.int32(0), jnp.int32(0)
        for g in range(n):
            lends = (counts[d] == 0) & (counts[g] == 2) & (ids[0, d] == ids[1, g])
            partner = partner + jnp.where(lends, g, 0)
            helps = (counts[g] == 0) & (counts[d] == 2) & (ids[0, g] == ids[1, d])
            helper = helper + jnp.where(helps, g, 0)
        ids[2, d] = partner
        ids[3, d] = helper
        slot = jnp.where(counts[d] == 0, 1, 0)
        group = jnp.where(counts[d] == 0, partner, d)
        for e in range(experts):
            rv[d, e] = router[slot, e, group]

    loop(0, n, pair)

    for k in (0, 1):
        upfull[k] = upstream_rows(k, core)

    up_swap.wait()
    for k in (0, 1):
        upfull[k] = (upfull[k].astype(f32) + uprecv[k].astype(f32)).astype(bf16)

    def keeper(i):
        return lax.rem(i + half * core, n)

    kept = lax.rem(z + half * core, n)
    keeps = kept < TILES

    def scatter_copy(i):
        rows = pl.ds(pl.multiple_of(i * 16, 16), 16)
        return remote(
            upfull.at[1, rows], up1.at[z], u1_send.at[i], u1_recv.at[z], {"dp": keeper(i)}
        )

    def scatter(i):
        @pl.when(keeper(i) != z)
        def _():
            scatter_copy(i).start()

        @pl.when(keeper(i) == z)
        def _():
            up1[z] = upfull[1, pl.ds(pl.multiple_of(i * 16, 16), 16)]

    loop(0, TILES, scatter)

    def order(v):
        return lax.rem(v - z + half + 1 + n, n)

    def tile_copy(k, b):
        to = lax.rem(place + k, PLANE)
        some = pl.ds(*BATCHES[b])
        return remote(
            tokbuf.at[tile, some], tokbuf.at[tile, some],
            tp_send.at[b, k], tp_recv.at[b, tile], on_plane(to, core),
        )

    @pl.when(serves)
    def _():
        loop(1, n, lambda k: token_copy(k).wait_recv())
        own_tokens.wait()

        def choose(v):
            lent, own = zrecv[ids[2, v], 1], zrecv[v, 0]
            tokbuf[tile, order(v)] = jnp.where(counts[v] == 0, lent, own)

        loop(0, n, choose)
        loop(1, PLANE, lambda k: tile_copy(k, 0).start())

    def pass_block(e, w):
        return remote(
            raw.at[core, e, w], raw.at[core, e, w], s_send.at[e, w], s_recv.at[e, w], sibling
        )

    for w in (0, 1):
        own_weights(w).wait()
        pass_block(expert, w).start()

    def pass_weights(k):
        e = lax.rem(expert + experts - k, experts)
        for w in (0, 1):
            remote(
                stored[w].at[0], raw.at[core, e, w], w_send.at[k, w], w_recv.at[k, w], sibling
            ).wait_recv()
            pass_block(e, w).start()

    loop(1, experts, pass_weights)

    @pl.when(serves)
    def _():
        loop(1, PLANE, lambda k: tile_copy(k, 1).start())


    def gather_copy(k):
        to = lax.rem(z + k, n)
        rows = pl.ds(pl.multiple_of(kept * 16, 16), 16)
        return remote(up2.at[to], upmoved.at[rows], u2_send.at[k], u2_recv.at[kept], {"dp": to})

    @pl.when(keeps)
    def _():
        def await_scatter(k):
            g = lax.rem(z + k, n)
            remote(
                up2.at[0], up1.at[g], u1_send.at[0], u1_recv.at[g], {"dp": right}
            ).wait_recv()

        loop(1, n, await_scatter)

        def lend(d):
            up2[d] = up1[ids[2, d]]

        loop(0, n, lend)
        loop(1, n, lambda k: gather_copy(k).start())
        upmoved[pl.ds(pl.multiple_of(kept * 16, 16), 16)] = up2[z]

    def await_weights(e):
        for w in (0, 1):
            remote(
                raw.at[core, e, w], raw.at[1 - core, e, w], s_send.at[e, w], s_recv.at[e, w], sibling
            ).wait_recv()

    loop(0, experts, await_weights)

    def await_tiles(b):
        some = pl.ds(*BATCHES[b])

        def await_tile(t):
            @pl.when(t != tile)
            def _():
                remote(
                    tokbuf.at[t, some], tokbuf.at[t, some], tp_send.at[b, 0], tp_recv.at[b, t], sibling
                ).wait_recv()

        loop(0, TILES, await_tile)

    await_tiles(0)

    def merge(v):
        weights = [rv[v, e] for e in range(experts)]

        def block(s, w, src, dst):
            total = weights[0] * raw[s, 0, w, src].astype(f32)
            for e in range(1, experts):
                total = total + weights[e] * raw[s, e, w, src].astype(f32)
            merged[v, dst] = total.astype(bf16)

        def tiles(q):
            for s in (0, 1):
                for w in (0, 1):
                    block(
                        s,
                        w,
                        pl.ds(pl.multiple_of(q * 64, 64), 64),
                        pl.ds(pl.multiple_of(w * 512 + q * 128 + s * 64, 64), 64),
                    )

        loop(0, 3, tiles)
        for s in (0, 1):
            for w in (0, 1):
                block(s, w, pl.ds(192, 32), pl.ds(384 + w * 64 + s * 32, 32))

    def tok(v):
        return tokbuf[:, order(v)].reshape(ROWS, 128)

    def partial(v):
        return lax.dot_general(tok(v), merged[v], NT, preferred_element_type=f32)

    def rs_copy(way, d, p):
        rows = pl.ds(*PIECES[p])
        return remote(
            inbox.at[way, d, rows], inbox.at[way, d - 1, rows],
            rs_send.at[way, p], rs_recv.at[way, d - 1, p], {"dp": towards[way]},
        )

    def ag_copy(way, d, p, v):
        rows = pl.ds(*PIECES[p])
        return remote(
            spread.at[v, rows], spread.at[v, rows],
            ag_send.at[way, d - 1, p], ag_recv.at[way, d - 1, p], {"dp": towards[way]},
        )

    def start_pieces(d, way):
        longer = (0, 1) if way == 0 else (2, 3)
        return longer if d == half else tuple(p for p in range(4) if p not in longer)

    far = ahead(0, half)
    merge(far)
    first = partial(far).astype(bf16)
    for way in (0, 1):
        for p in start_pieces(half, way):
            at, size = PIECES[p]
            inbox[way, half, at : at + size] = first[at : at + size]
            rs_copy(way, half, p).start()
    for way in (0, 1):
        v = ahead(way, half - 1)
        merge(v)
        contrib[(half - 1) % 2, way] = partial(v)
        for p in start_pieces(half - 1, way):
            rows = pl.ds(*PIECES[p])
            inbox[way, half - 1, rows] = contrib[(half - 1) % 2, way, rows].astype(bf16)
            rs_copy(way, half - 1, p).start()
    await_tiles(1)

    def pass_on(way, d, p):
        rows = pl.ds(*PIECES[p])
        rs_copy(way, d + 1, p).wait_recv()
        total = inbox[way, d, rows].astype(f32) + contrib[lax.rem(d, 2), way, rows]
        inbox[way, d, rows] = total.astype(bf16)
        rs_copy(way, d, p).start()

    def prepare(d, i):
        way, second = i // 2, i % 2
        v = ahead(way, d)
        if second:
            contrib[lax.rem(d, 2), way] = partial(v)
        else:
            merge(v)

    for i in range(4):
        if i < 2:
            pass_on(0, half - 1, start_pieces(half, 0)[i])
            pass_on(1, half - 1, start_pieces(half, 1)[i])
        prepare(half - 2, i)

    def rs_step(i):
        d = half - 2 - i
        for j, (up, down) in enumerate(((2, 0), (3, 1), (0, 2), (1, 3))):
            pass_on(0, d, up)
            pass_on(1, d, down)
            prepare(d - 1, j)

    loop(0, half - 2, rs_step)

    def await_gather(i):
        @pl.when(i != kept)
        def _():
            rows = pl.ds(pl.multiple_of(i * 16, 16), 16)
            remote(
                up2.at[0], upmoved.at[rows], u2_send.at[0], u2_recv.at[i], {"dp": right}
            ).wait_recv()

    loop(0, TILES, await_gather)

    def gate_part(gate, up, flowing):
        s = jax.nn.sigmoid(gate)
        return (flowing * up * s * (1.0 + gate * (1.0 - s))).astype(bf16)

    def up_part(gate, flowing):
        return (flowing * gate * jax.nn.sigmoid(gate)).astype(bf16)

    for p in range(4):
        rows = pl.ds(*PIECES[p])
        for way in (0, 1):
            rs_copy(way, 1, p).wait_recv()
        pre = inbox[0, 0, rows].astype(f32) + inbox[1, 0, rows].astype(f32) + contrib[0, 0, rows]
        flowing = jnp.where(counts[z] == 0, upmoved[rows], upfull[0, rows]).astype(f32)
        gate, mixed, up = pre[:, :384], pre[:, 384:512], pre[:, 512:]
        spread[z, rows, :384] = gate_part(gate, up, flowing[:, :384])
        spread[z, rows, 512:] = up_part(gate, flowing[:, :384])
        low = lax.broadcasted_iota(jnp.int32, mixed.shape, 1) < 64
        rolled = pltpu.roll(mixed, 64, 1)
        gate, up = jnp.where(low, mixed, rolled), jnp.where(low, rolled, mixed)
        spread[z, rows, 384:512] = jnp.where(
            low, gate_part(gate, up, flowing[:, 384:]), up_part(gate, flowing[:, 384:])
        )
        for way in (0, 1):
            ag_copy(way, 1, p, z).start()

    acc[...] = jnp.zeros_like(acc)

    wide = lax.broadcasted_iota(jnp.int32, (PLANE * 16, ROWS), 0)
    slim = lax.broadcasted_iota(jnp.int32, (PLANE * 16, ROWS), 1)
    spare = (wide & 15) < TILES
    widen = (spare & (slim == (wide >> 4) * TILES + (wide & 15))).astype(f32).astype(bf16)
    my_block = x * 4 + y_hi * 2 + core

    def back(owners, i, unit):
        rows, hidden = pl.ds(*PIECES[i]), pl.ds(*PARTS[i])
        terms = []
        for j, v in enumerate(owners):
            term[j, rows] = jnp.dot(
                spread[v, rows], merged[v], preferred_element_type=f32
            ).astype(bf16)
            terms.append(
                lax.dot_general(spread[v, :, hidden], tok(v), TN, preferred_element_type=f32)
            )
            if i == 3:
                blocks = jnp.dot(widen, term[j], preferred_element_type=f32).astype(bf16)
                tg_out[:, unit + j] = blocks.reshape(PLANE, 16, 128)
        for e in range(experts):
            total = acc[e, hidden]
            for v, t in zip(owners, terms):
                total = total + rv[v, e] * t
            acc[e, hidden] = total
        if i == 3:
            send_terms(unit, len(owners))

    def term_copy(k, units):
        where = {"y_lo": core, "x": k // 4, "y_hi": lax.rem(k // 2, 2), "core": lax.rem(k, 2)}
        return remote(
            tg_out.at[k, units], tg_in.at[place, units], gp_send.at[k], gp_recv.at[place], where
        )

    def send_terms(unit, count):
        units = pl.ds(unit, count)

        def send(k):
            here = (y_lo == core) & (k == my_block)

            @pl.when(here)
            def _():
                tg_in[place, units] = tg_out[k, units]

            @pl.when(jnp.logical_not(here))
            def _():
                term_copy(k, units).start()

        loop(0, PLANE, send)

    def receive(way, d, p):
        ag_copy(way, d, p, behind(way, d)).wait_recv()

    def forward(way, d, p):
        ag_copy(way, d + 1, p, behind(way, d)).start()

    def ag_step(d, owners, last, unit):
        for p in range(4):
            for way in (0, 1):
                receive(way, d, p)
                if not last or p in start_pieces(half, way):
                    forward(way, d, p)
            back(owners, p, unit)

    ag_step(1, (z,), False, 0)
    loop(
        2,
        half - 1,
        lambda d: ag_step(d, (behind(0, d - 1), behind(1, d - 1)), False, 2 * d - 3),
    )
    ag_step(half - 1, (behind(0, half - 2), behind(1, half - 2)), True, n - 5)
    for i in range(4):
        back((behind(0, half - 1), behind(1, half - 1)), i, n - 3)

    for way in (0, 1):
        for p in range(4):
            reach = half if p in start_pieces(half, way) else half - 1
            started = inbox.at[way, pl.ds(1, reach), pl.ds(*PIECES[p])]
            remote(
                started, started, rs_send.at[way, p], rs_recv.at[way, 0, p], sibling
            ).wait_send()

    @pl.when(serves)
    def _():
        loop(1, n, lambda k: token_copy(k).wait_send())
        for b in (0, 1):
            loop(1, PLANE, lambda k, b=b: tile_copy(k, b).wait_send())

    def weights_sent(k):
        for w in (0, 1):
            weight_copy(k, w).wait_send()

    loop(1, experts, weights_sent)

    def passed(e):
        for w in (0, 1):
            pass_block(e, w).wait_send()

    loop(0, experts, passed)

    def scattered(i):
        @pl.when(keeper(i) != z)
        def _():
            scatter_copy(i).wait_send()

    loop(0, TILES, scattered)

    @pl.when(keeps)
    def _():
        loop(1, n, lambda k: gather_copy(k).wait_send())

    for way in (0, 1):
        for p in start_pieces(half, way):
            receive(way, half, p)
    for i in range(4):
        back((far,), i, n - 1)

    other = 1 - core

    def units_of(w, s):
        for q in range(3):
            yield q * 64, 64, pl.ds(pl.multiple_of(w * 512 + q * 128 + s * 64, 64), 64)
        yield 192, 32, pl.ds(pl.multiple_of(384 + w * 64 + s * 32, 32), 32)

    def cross_copy(e):
        return remote(sib_out.at[e], sib_in.at[e], x_send.at[e], x_recv.at[e], sibling)

    def cross(e):
        for w in (0, 1):
            for at, size, hidden in units_of(w, other):
                sib_out[e, w, at : at + size] = acc[e, hidden].astype(bf16)
        cross_copy(e).start()

    loop(1, experts + 1, lambda k: cross(lax.rem(expert + k, experts)))

    outs = (out_gate, out_up)

    def home_copy(k, w):
        to = lax.rem(expert + k, experts)
        return remote(
            wg_out.at[to, w], outs[w].at[expert], e_send.at[k, w], e_recv.at[k, w], on_expert(to)
        )

    def own_home(w):
        return pltpu.make_async_copy(wg_out.at[expert, w], outs[w].at[expert], local_sem.at[w])

    def settle(k):
        e = lax.rem(expert + k, experts)
        cross_copy(e).wait_recv()
        for w in (0, 1):
            for at, size, hidden in units_of(w, core):
                total = acc[e, hidden] + sib_in[e, w, at : at + size].astype(f32)
                wg_out[e, w, at : at + size] = total.astype(bf16)

        @pl.when(k < experts)
        def _():
            for w in (0, 1):
                home_copy(k, w).start()

    loop(1, experts + 1, settle)
    for w in (0, 1):
        own_home(w).start()

    def await_terms(q):
        @pl.when(jnp.logical_not((y_lo == core) & (q == place)))
        def _():
            remote(
                tg_in.at[q], tg_in.at[q], gp_send.at[0], gp_recv.at[q], sibling
            ).wait_recv()

    loop(0, PLANE, await_terms)
    sums = tg_in[0].astype(f32)
    for q in range(1, PLANE):
        sums = sums + tg_in[q].astype(f32)
    term_sum = tg_out.at[0]

    def await_sent(k):
        @pl.when(jnp.logical_not((y_lo == core) & (k == my_block)))
        def _():
            remote(
                tg_out.at[k], tg_in.at[0], gp_send.at[k], gp_recv.at[0], sibling
            ).wait_send()

    loop(0, PLANE, await_sent)
    term_sum[...] = sums.astype(bf16)

    def unit_of(v):
        apart = lax.rem(v - z + n, n)
        near = jnp.where(apart < half, 2 * apart, 2 * (n - apart) - 1)
        return jnp.where(apart == half, n - 1, near)

    def slots(g):
        nothing = jnp.zeros((16, 128), bf16)
        first, second = term_sum[unit_of(g)], term_sum[unit_of(ids[3, g])]
        tg_send[g, 0] = jnp.where(counts[g] == 0, nothing, first)
        tg_send[g, 1] = jnp.where(counts[g] == 2, second, nothing)

    loop(0, n, slots)

    def slot_copy(k):
        to = lax.rem(z + k, n)
        return remote(tg_send.at[to], tg_fin.at[z], gz_send.at[k], gz_recv.at[k], {"dp": to})

    loop(1, n, lambda k: slot_copy(k).start())
    tg_fin[z] = tg_send[z]

    for way in (0, 1):
        for p in range(4):
            reach = half if p in start_pieces(half, way) else half - 1
            loop(1, reach + 1, lambda d, way=way, p=p: ag_copy(way, d, p, 0).wait_send())
    loop(0, experts, lambda e: cross_copy(e).wait_send())

    def home(k):
        for w in (0, 1):
            home_copy(k, w).wait()

    loop(1, experts, home)
    for w in (0, 1):
        own_home(w).wait()
    loop(1, n, lambda k: slot_copy(k).wait())
    out_tokens[...] = tg_fin[...]


def finish_kernel(gate, up, out_gate, out_up, sems):
    pieces = sems.shape[1]
    size = gate.shape[0] // pieces
    for go in (True, False):
        for w, (src, dst) in enumerate(((gate, out_gate), (up, out_up))):
            for i in range(pieces):
                some = pl.ds(i * size, size)
                copy = pltpu.make_async_copy(src.at[some], dst.at[some], sems.at[w, i])
                copy.start() if go else copy.wait()


def local(tokens, upstream, router, counts, w_gate, w_up):
    n = lax.axis_size("dp")
    _, slots, seg_len, width = tokens.shape
    _, depth, blocks, cols = w_gate.shape
    experts = router.shape[2]
    half = n // 2
    hidden = 4 * cols
    vmem, smem, hbm = (
        pl.BlockSpec(memory_space=space) for space in (pltpu.VMEM, pltpu.SMEM, pl.ANY)
    )
    dma = pltpu.SemaphoreType.DMA
    home = jax.ShapeDtypeStruct((blocks, cols, depth), bf16)
    tg, gate_grad, up_grad = pl.pallas_call(
        functools.partial(kernel, n),
        out_shape=(jax.ShapeDtypeStruct((n, slots, 16, depth), bf16), home, home),
        in_specs=[smem, smem, hbm, hbm, hbm, vmem],
        out_specs=(vmem, hbm, hbm),
        scratch_shapes=[
            pltpu.SMEM((4, n), jnp.int32),
            pltpu.SMEM((n, experts), f32),
            pltpu.VMEM((2, experts, 2, cols, depth), bf16),
            pltpu.VMEM((n, slots, 16, depth), bf16),
            pltpu.VMEM((TILES, n, 16, depth), bf16),
            pltpu.VMEM((slots, ROWS, 512), bf16),
            pltpu.VMEM((slots, ROWS, 512), bf16),
            pltpu.VMEM((slots, ROWS, 512), bf16),
            pltpu.VMEM((n, 16, 512), bf16),
            pltpu.VMEM((n, 16, 512), bf16),
            pltpu.VMEM((ROWS, 512), bf16),
            pltpu.VMEM((n, hidden, depth), bf16),
            pltpu.VMEM((2, 2, ROWS, hidden), f32),
            pltpu.VMEM((2, half + 1, ROWS, hidden), bf16),
            pltpu.VMEM((n, ROWS, hidden), bf16),
            pltpu.VMEM((experts, hidden, depth), f32),
            pltpu.VMEM((2, ROWS, depth), bf16),
            pltpu.VMEM((PLANE, n, 16, depth), bf16),
            pltpu.VMEM((PLANE, n, 16, depth), bf16),
            pltpu.VMEM((n, slots, 16, depth), bf16),
            pltpu.VMEM((n, slots, 16, depth), bf16),
            pltpu.VMEM((experts, 2, cols, depth), bf16),
            pltpu.VMEM((experts, 2, cols, depth), bf16),
            pltpu.VMEM((experts, 2, cols, depth), bf16),
            dma((3,)),
            dma((experts, 2)), dma((experts, 2)),
            dma((experts, 2)), dma((experts, 2)),
            dma((n,)), dma((n,)),
            dma((2, PLANE)), dma((2, TILES)),
            dma((2,)),
            dma((TILES,)), dma((n,)),
            dma((n,)), dma((PLANE,)),
            dma((2, 4)), dma((2, half, 4)),
            dma((2, half, 4)), dma((2, half, 4)),
            dma((PLANE,)), dma((PLANE,)),
            dma((n,)), dma((n,)),
            dma((experts,)), dma((experts,)),
            dma((experts, 2)), dma((experts, 2)),
        ],
        compiler_params=pltpu.CompilerParams(
            collective_id=0, has_side_effects=True, vmem_limit_bytes=56 * 2**20
        ),
    )(
        counts,
        router.transpose(1, 2, 0),
        w_gate[0].transpose(1, 2, 0),
        w_up[0].transpose(1, 2, 0),
        tokens[0],
        upstream[0].transpose(0, 2, 1),
    )
    gate_grad, up_grad = pl.pallas_call(
        finish_kernel,
        out_shape=(home, home),
        in_specs=[vmem, vmem],
        out_specs=(hbm, hbm),
        scratch_shapes=[dma((2, 4))],
    )(gate_grad, up_grad)
    tokens_grad = tg[:, :, : seg_len // 32].transpose(1, 2, 0, 3).reshape(1, slots, -1, width)
    return (tokens_grad, gate_grad.transpose(2, 0, 1)[None], up_grad.transpose(2, 0, 1)[None])


def solution(mesh):
    shape = (mesh.shape["dp"], 2, mesh.shape["expert"] // 2, mesh.shape["tensor"] // 2, 2)
    fine = Mesh(mesh.devices.reshape(shape), ("dp", "y_lo", "x", "y_hi", "core"))
    tensor = ("y_hi", "core")
    weights = P(EXPERT, "dp", None, tensor)
    in_specs = (
        P("dp", None, None, None),
        P("dp", None, None, EXPERT + tensor),
        P(),
        P(),
        weights,
        weights,
    )
    out_specs = (P("dp", None, EXPERT + tensor, None), weights, weights)
    return jax.shard_map(local, mesh=fine, in_specs=in_specs, out_specs=out_specs, check_vma=False)
```

```python
import functools

import jax
import jax.numpy as jnp
from jax import lax
from jax.experimental import pallas as pl
from jax.experimental.pallas import tpu as pltpu
from jax.sharding import Mesh, PartitionSpec as P

MESH = pl.DeviceIdType.MESH
EXPERT = ("y_lo", "x")
PLANE = 16
ROWS = 176
TILES = 11
COLS = 224
PIECES = ((0, 48), (48, 48), (96, 48), (144, 32))
BATCHES = ((0, 3), (3, 13))
PARTS = ((0, 256), (256, 256), (512, 256), (768, 128))
NT = (((1,), (1,)), ((), ()))
TN = (((0,), (0,)), ((), ()))
f32, bf16 = jnp.float32, jnp.bfloat16


def loop(lo, hi, body):
    def step(i, carry):
        body(i)
        return carry

    lax.fori_loop(lo, hi, step, 0)


def kernel(
    n, counts, router, w_gate, w_up, tokens, upstream,
    out_tokens, out_gate, out_up,
    ids, rv, raw, zrecv, tokbuf, upsend, uprecv, upfull, up1, up2, upmoved,
    merged, contrib, inbox, spread, acc,
    term, tg_out, tg_in, tg_send, tg_fin, sib_out, sib_in, wg_out,
    local_sem, w_send, w_recv, s_send, s_recv, tz_send, tz_recv, tp_send, tp_recv,
    us_sem, u1_send, u1_recv, u2_send, u2_recv,
    rs_send, rs_recv, ag_send, ag_recv,
    gp_send, gp_recv, gz_send, gz_recv, x_send, x_recv, e_send, e_recv,
):
    z = lax.axis_index("dp")
    y_lo, x, y_hi = lax.axis_index("y_lo"), lax.axis_index("x"), lax.axis_index("y_hi")
    core = lax.axis_index("core")
    expert = y_lo * 4 + x
    place = expert * 2 + y_hi
    half = n // 2
    experts = raw.shape[1]
    right, left = lax.rem(z + 1, n), lax.rem(z + n - 1, n)
    towards = (right, left)

    def on_plane(q, c):
        return {"y_lo": q // 8, "x": lax.rem(q // 2, 4), "y_hi": lax.rem(q, 2), "core": c}

    def on_expert(e):
        return {"y_lo": e // 4, "x": lax.rem(e, 4)}

    sibling = {"core": 1 - core}

    def remote(src, dst, send, recv, where):
        return pltpu.make_async_remote_copy(
            src_ref=src, dst_ref=dst, send_sem=send, recv_sem=recv,
            device_id=where, device_id_type=MESH,
        )

    def ahead(way, d):
        return lax.rem(z + d, n) if way == 0 else lax.rem(z + n - d, n)

    def behind(way, d):
        return ahead(1 - way, d)

    barrier = pltpu.get_barrier_semaphore()

    def greet(where):
        pl.semaphore_signal(barrier, inc=1, device_id=where, device_id_type=MESH)

    greet(sibling)
    loop(1, n, lambda k: greet({"dp": lax.rem(z + k, n)}))

    def greet_chip(k):
        q = lax.rem(place + k, PLANE)
        greet(on_plane(q, 0))
        greet(on_plane(q, 1))

    loop(1, PLANE, greet_chip)
    pl.semaphore_wait(barrier, 1 + (n - 1) + 2 * (PLANE - 1))

    tile = lax.rem(place + TILES * core, PLANE)
    serves = tile < TILES

    def token_block(to):
        rows = pl.ds(pl.multiple_of(core * ROWS + tile * 16, 16), 16)
        return tokens.at[:, rows, pl.ds(pl.multiple_of(to * 128, 128), 128)]

    def token_copy(k):
        to = lax.rem(z + k, n)
        return remote(token_block(to), zrecv.at[z], tz_send.at[k], tz_recv.at[k], {"dp": to})

    own_tokens = pltpu.make_async_copy(token_block(z), zrecv.at[z], local_sem.at[2])

    @pl.when(serves)
    def _():
        loop(1, n, lambda k: token_copy(k).start())
        own_tokens.start()

    stored = (w_gate, w_up)

    def weight_copy(k, w):
        to = lax.rem(expert + k, experts)
        return remote(
            stored[w].at[to], raw.at[core, expert, w], w_send.at[k, w], w_recv.at[k, w], on_expert(to)
        )

    def own_weights(w):
        return pltpu.make_async_copy(stored[w].at[expert], raw.at[core, expert, w], local_sem.at[w])

    for w in (0, 1):
        own_weights(w).start()

    def send_weights(k):
        for w in (0, 1):
            weight_copy(k, w).start()

    loop(1, experts, send_weights)

    row = lax.broadcasted_iota(jnp.int32, (ROWS, 2 * ROWS), 0)
    col = lax.broadcasted_iota(jnp.int32, (ROWS, 2 * ROWS), 1)
    unit = lax.broadcasted_iota(jnp.int32, (COLS, 512), 0)
    lane = lax.broadcasted_iota(jnp.int32, (COLS, 512), 1)
    tail = unit >= 192
    spot = jnp.where(
        tail, unit + (192 + 32 * core), (unit >> 6) * 128 + (unit & 63) + 64 * core
    )
    put = ((lane == spot) | (tail & (lane == spot + 64))).astype(f32).astype(bf16)

    def upstream_rows(k, which):
        pick = (col == row + ROWS * which).astype(f32).astype(bf16)
        turned = lax.dot_general(pick, upstream[k], NT, preferred_element_type=f32)
        return jnp.dot(turned.astype(bf16), put, preferred_element_type=f32).astype(bf16)

    for k in (0, 1):
        upsend[k] = upstream_rows(k, 1 - core)
    up_swap = remote(upsend, uprecv, us_sem.at[0], us_sem.at[1], sibling)
    up_swap.start()

    def ranks(g, carry):
        empties, doubles = carry
        ids[0, g] = empties
        ids[1, g] = doubles
        held = counts[g]
        return (
            empties + jnp.where(held == 0, 1, 0),
            doubles + jnp.where(held == 2, 1, 0),
        )

    lax.fori_loop(0, n, ranks, (jnp.int32(0), jnp.int32(0)))

    def pair(d):
        partner, helper = jnp.int32(0), jnp.int32(0)
        for g in range(n):
            lends = (counts[d] == 0) & (counts[g] == 2) & (ids[0, d] == ids[1, g])
            partner = partner + jnp.where(lends, g, 0)
            helps = (counts[g] == 0) & (counts[d] == 2) & (ids[0, g] == ids[1, d])
            helper = helper + jnp.where(helps, g, 0)
        ids[2, d] = partner
        ids[3, d] = helper
        slot = jnp.where(counts[d] == 0, 1, 0)
        group = jnp.where(counts[d] == 0, partner, d)
        for e in range(experts):
            rv[d, e] = router[slot, e, group]

    loop(0, n, pair)

    for k in (0, 1):
        upfull[k] = upstream_rows(k, core)

    up_swap.wait()
    for k in (0, 1):
        upfull[k] = (upfull[k].astype(f32) + uprecv[k].astype(f32)).astype(bf16)

    def keeper(i):
        return lax.rem(i + half * core, n)

    kept = lax.rem(z + half * core, n)
    keeps = kept < TILES

    def scatter_copy(i):
        rows = pl.ds(pl.multiple_of(i * 16, 16), 16)
        return remote(
            upfull.at[1, rows], up1.at[z], u1_send.at[i], u1_recv.at[z], {"dp": keeper(i)}
        )

    def scatter(i):
        @pl.when(keeper(i) != z)
        def _():
            scatter_copy(i).start()

        @pl.when(keeper(i) == z)
        def _():
            up1[z] = upfull[1, pl.ds(pl.multiple_of(i * 16, 16), 16)]

    loop(0, TILES, scatter)

    def order(v):
        return lax.rem(v - z + half + 1 + n, n)

    def tile_copy(k, b):
        to = lax.rem(place + k, PLANE)
        some = pl.ds(*BATCHES[b])
        return remote(
            tokbuf.at[tile, some], tokbuf.at[tile, some],
            tp_send.at[b, k], tp_recv.at[b, tile], on_plane(to, core),
        )

    @pl.when(serves)
    def _():
        loop(1, n, lambda k: token_copy(k).wait_recv())
        own_tokens.wait()

        def choose(v):
            lent, own = zrecv[ids[2, v], 1], zrecv[v, 0]
            tokbuf[tile, order(v)] = jnp.where(counts[v] == 0, lent, own)

        loop(0, n, choose)
        loop(1, PLANE, lambda k: tile_copy(k, 0).start())

    def pass_block(e, w):
        return remote(
            raw.at[core, e, w], raw.at[core, e, w], s_send.at[e, w], s_recv.at[e, w], sibling
        )

    for w in (0, 1):
        own_weights(w).wait()
        pass_block(expert, w).start()

    def pass_weights(k):
        e = lax.rem(expert + experts - k, experts)
        for w in (0, 1):
            remote(
                stored[w].at[0], raw.at[core, e, w], w_send.at[k, w], w_recv.at[k, w], sibling
            ).wait_recv()
            pass_block(e, w).start()

    loop(1, experts, pass_weights)


    def await_weights(e):
        for w in (0, 1):
            remote(
                raw.at[core, e, w], raw.at[1 - core, e, w], s_send.at[e, w], s_recv.at[e, w], sibling
            ).wait_recv()

    loop(0, experts, await_weights)

    def await_tiles(b):
        some = pl.ds(*BATCHES[b])

        def await_tile(t):
            @pl.when(t != tile)
            def _():
                remote(
                    tokbuf.at[t, some], tokbuf.at[t, some], tp_send.at[b, 0], tp_recv.at[b, t], sibling
                ).wait_recv()

        loop(0, TILES, await_tile)

    await_tiles(0)

    def merge(v):
        weights = [rv[v, e] for e in range(experts)]

        def block(s, w, src, dst):
            total = weights[0] * raw[s, 0, w, src].astype(f32)
            for e in range(1, experts):
                total = total + weights[e] * raw[s, e, w, src].astype(f32)
            merged[v, dst] = total.astype(bf16)

        def tiles(q):
            for s in (0, 1):
                for w in (0, 1):
                    block(
                        s,
                        w,
                        pl.ds(pl.multiple_of(q * 64, 64), 64),
                        pl.ds(pl.multiple_of(w * 512 + q * 128 + s * 64, 64), 64),
                    )

        loop(0, 3, tiles)
        for s in (0, 1):
            for w in (0, 1):
                block(s, w, pl.ds(192, 32), pl.ds(384 + w * 64 + s * 32, 32))

    def tok(v):
        return tokbuf[:, order(v)].reshape(ROWS, 128)

    def partial(v):
        return lax.dot_general(tok(v), merged[v], NT, preferred_element_type=f32)

    def rs_copy(way, d, p):
        rows = pl.ds(*PIECES[p])
        return remote(
            inbox.at[way, d, rows], inbox.at[way, d - 1, rows],
            rs_send.at[way, p], rs_recv.at[way, d - 1, p], {"dp": towards[way]},
        )

    def ag_copy(way, d, p, v):
        rows = pl.ds(*PIECES[p])
        return remote(
            spread.at[v, rows], spread.at[v, rows],
            ag_send.at[way, d - 1, p], ag_recv.at[way, d - 1, p], {"dp": towards[way]},
        )

    def start_pieces(d, way):
        longer = (0, 1) if way == 0 else (2, 3)
        return longer if d == half else tuple(p for p in range(4) if p not in longer)

    far = ahead(0, half)
    merge(far)
    first = partial(far).astype(bf16)
    for way in (0, 1):
        for p in start_pieces(half, way):
            at, size = PIECES[p]
            inbox[way, half, at : at + size] = first[at : at + size]
            rs_copy(way, half, p).start()

    @pl.when(serves)
    def _():
        loop(1, PLANE, lambda k: tile_copy(k, 1).start())

    for way in (0, 1):
        v = ahead(way, half - 1)
        merge(v)
        contrib[(half - 1) % 2, way] = partial(v)
        for p in start_pieces(half - 1, way):
            rows = pl.ds(*PIECES[p])
            inbox[way, half - 1, rows] = contrib[(half - 1) % 2, way, rows].astype(bf16)
            rs_copy(way, half - 1, p).start()
    def gather_copy(k):
        to = lax.rem(z + k, n)
        rows = pl.ds(pl.multiple_of(kept * 16, 16), 16)
        return remote(up2.at[to], upmoved.at[rows], u2_send.at[k], u2_recv.at[kept], {"dp": to})

    @pl.when(keeps)
    def _():
        def await_scatter(k):
            g = lax.rem(z + k, n)
            remote(
                up2.at[0], up1.at[g], u1_send.at[0], u1_recv.at[g], {"dp": right}
            ).wait_recv()

        loop(1, n, await_scatter)

        def lend(d):
            up2[d] = up1[ids[2, d]]

        loop(0, n, lend)
        loop(1, n, lambda k: gather_copy(k).start())
        upmoved[pl.ds(pl.multiple_of(kept * 16, 16), 16)] = up2[z]

    await_tiles(1)

    def pass_on(way, d, p):
        rows = pl.ds(*PIECES[p])
        rs_copy(way, d + 1, p).wait_recv()
        total = inbox[way, d, rows].astype(f32) + contrib[lax.rem(d, 2), way, rows]
        inbox[way, d, rows] = total.astype(bf16)
        rs_copy(way, d, p).start()

    def prepare(d, i):
        way, second = i // 2, i % 2
        v = ahead(way, d)
        if second:
            contrib[lax.rem(d, 2), way] = partial(v)
        else:
            merge(v)

    for i in range(4):
        if i < 2:
            pass_on(0, half - 1, start_pieces(half, 0)[i])
            pass_on(1, half - 1, start_pieces(half, 1)[i])
        prepare(half - 2, i)

    def rs_step(i):
        d = half - 2 - i
        for j, (up, down) in enumerate(((2, 0), (3, 1), (0, 2), (1, 3))):
            pass_on(0, d, up)
            pass_on(1, d, down)
            prepare(d - 1, j)

    loop(0, half - 2, rs_step)

    def await_gather(i):
        @pl.when(i != kept)
        def _():
            rows = pl.ds(pl.multiple_of(i * 16, 16), 16)
            remote(
                up2.at[0], upmoved.at[rows], u2_send.at[0], u2_recv.at[i], {"dp": right}
            ).wait_recv()

    loop(0, TILES, await_gather)

    def gate_part(gate, up, flowing):
        s = jax.nn.sigmoid(gate)
        return (flowing * up * s * (1.0 + gate * (1.0 - s))).astype(bf16)

    def up_part(gate, flowing):
        return (flowing * gate * jax.nn.sigmoid(gate)).astype(bf16)

    for p in range(4):
        rows = pl.ds(*PIECES[p])
        for way in (0, 1):
            rs_copy(way, 1, p).wait_recv()
        pre = inbox[0, 0, rows].astype(f32) + inbox[1, 0, rows].astype(f32) + contrib[0, 0, rows]
        flowing = jnp.where(counts[z] == 0, upmoved[rows], upfull[0, rows]).astype(f32)
        gate, mixed, up = pre[:, :384], pre[:, 384:512], pre[:, 512:]
        spread[z, rows, :384] = gate_part(gate, up, flowing[:, :384])
        spread[z, rows, 512:] = up_part(gate, flowing[:, :384])
        low = lax.broadcasted_iota(jnp.int32, mixed.shape, 1) < 64
        rolled = pltpu.roll(mixed, 64, 1)
        gate, up = jnp.where(low, mixed, rolled), jnp.where(low, rolled, mixed)
        spread[z, rows, 384:512] = jnp.where(
            low, gate_part(gate, up, flowing[:, 384:]), up_part(gate, flowing[:, 384:])
        )
        for way in (0, 1):
            ag_copy(way, 1, p, z).start()

    acc[...] = jnp.zeros_like(acc)

    wide = lax.broadcasted_iota(jnp.int32, (PLANE * 16, ROWS), 0)
    slim = lax.broadcasted_iota(jnp.int32, (PLANE * 16, ROWS), 1)
    spare = (wide & 15) < TILES
    widen = (spare & (slim == (wide >> 4) * TILES + (wide & 15))).astype(f32).astype(bf16)
    my_block = x * 4 + y_hi * 2 + core

    def back(owners, i, unit):
        back_tokens(owners, i, unit)
        back_weights(owners, i)
        if i == 3:
            send_terms(unit, len(owners))

    def back_tokens(owners, i, unit):
        rows = pl.ds(*PIECES[i])
        for j, v in enumerate(owners):
            term[j, rows] = jnp.dot(
                spread[v, rows], merged[v], preferred_element_type=f32
            ).astype(bf16)
            if i == 3:
                blocks = jnp.dot(widen, term[j], preferred_element_type=f32).astype(bf16)
                tg_out[:, unit + j] = blocks.reshape(PLANE, 16, 128)

    def back_weights(owners, i):
        hidden = pl.ds(*PARTS[i])
        terms = [
            lax.dot_general(spread[v, :, hidden], tok(v), TN, preferred_element_type=f32)
            for v in owners
        ]
        for e in range(experts):
            total = acc[e, hidden]
            for v, t in zip(owners, terms):
                total = total + rv[v, e] * t
            acc[e, hidden] = total

    def term_copy(k, units):
        where = {"y_lo": core, "x": k // 4, "y_hi": lax.rem(k // 2, 2), "core": lax.rem(k, 2)}
        return remote(
            tg_out.at[k, units], tg_in.at[place, units], gp_send.at[k], gp_recv.at[place], where
        )

    def send_terms(unit, count):
        units = pl.ds(unit, count)

        def send(k):
            here = (y_lo == core) & (k == my_block)

            @pl.when(here)
            def _():
                tg_in[place, units] = tg_out[k, units]

            @pl.when(jnp.logical_not(here))
            def _():
                term_copy(k, units).start()

        loop(0, PLANE, send)

    def receive(way, d, p):
        ag_copy(way, d, p, behind(way, d)).wait_recv()

    def forward(way, d, p):
        ag_copy(way, d + 1, p, behind(way, d)).start()

    def ag_step(d, owners, last, unit):
        for p in range(4):
            for way in (0, 1):
                receive(way, d, p)
                if not last or p in start_pieces(half, way):
                    forward(way, d, p)
            back(owners, p, unit)

    ag_step(1, (z,), False, 0)
    loop(
        2,
        half - 1,
        lambda d: ag_step(d, (behind(0, d - 1), behind(1, d - 1)), False, 2 * d - 3),
    )
    ag_step(half - 1, (behind(0, half - 2), behind(1, half - 2)), True, n - 5)
    for i in range(4):
        back((behind(0, half - 1), behind(1, half - 1)), i, n - 3)

    for way in (0, 1):
        for p in range(4):
            reach = half if p in start_pieces(half, way) else half - 1
            started = inbox.at[way, pl.ds(1, reach), pl.ds(*PIECES[p])]
            remote(
                started, started, rs_send.at[way, p], rs_recv.at[way, 0, p], sibling
            ).wait_send()

    @pl.when(serves)
    def _():
        loop(1, n, lambda k: token_copy(k).wait_send())
        for b in (0, 1):
            loop(1, PLANE, lambda k, b=b: tile_copy(k, b).wait_send())

    def weights_sent(k):
        for w in (0, 1):
            weight_copy(k, w).wait_send()

    loop(1, experts, weights_sent)

    def passed(e):
        for w in (0, 1):
            pass_block(e, w).wait_send()

    loop(0, experts, passed)

    def scattered(i):
        @pl.when(keeper(i) != z)
        def _():
            scatter_copy(i).wait_send()

    loop(0, TILES, scattered)

    @pl.when(keeps)
    def _():
        loop(1, n, lambda k: gather_copy(k).wait_send())

    for way in (0, 1):
        for p in start_pieces(half, way):
            receive(way, half, p)
    for i in range(4):
        back_weights((far,), i)

    other = 1 - core

    def units_of(w, s):
        for q in range(3):
            yield q * 64, 64, pl.ds(pl.multiple_of(w * 512 + q * 128 + s * 64, 64), 64)
        yield 192, 32, pl.ds(pl.multiple_of(384 + w * 64 + s * 32, 32), 32)

    def cross_copy(e):
        return remote(sib_out.at[e], sib_in.at[e], x_send.at[e], x_recv.at[e], sibling)

    def cross(e):
        for w in (0, 1):
            for at, size, hidden in units_of(w, other):
                sib_out[e, w, at : at + size] = acc[e, hidden].astype(bf16)
        cross_copy(e).start()

    loop(1, experts + 1, lambda k: cross(lax.rem(expert + k, experts)))
    for i in range(4):
        back_tokens((far,), i, n - 1)
    send_terms(n - 1, 1)

    outs = (out_gate, out_up)

    def home_copy(k, w):
        to = lax.rem(expert + k, experts)
        return remote(
            wg_out.at[to, w], outs[w].at[expert], e_send.at[k, w], e_recv.at[k, w], on_expert(to)
        )

    def own_home(w):
        return pltpu.make_async_copy(wg_out.at[expert, w], outs[w].at[expert], local_sem.at[w])

    def settle(k):
        e = lax.rem(expert + k, experts)
        cross_copy(e).wait_recv()
        for w in (0, 1):
            for at, size, hidden in units_of(w, core):
                total = acc[e, hidden] + sib_in[e, w, at : at + size].astype(f32)
                wg_out[e, w, at : at + size] = total.astype(bf16)

        @pl.when(k < experts)
        def _():
            for w in (0, 1):
                home_copy(k, w).start()

    loop(1, experts + 1, settle)
    for w in (0, 1):
        own_home(w).start()

    def await_terms(q):
        @pl.when(jnp.logical_not((y_lo == core) & (q == place)))
        def _():
            remote(
                tg_in.at[q], tg_in.at[q], gp_send.at[0], gp_recv.at[q], sibling
            ).wait_recv()

    loop(0, PLANE, await_terms)
    sums = tg_in[0].astype(f32)
    for q in range(1, PLANE):
        sums = sums + tg_in[q].astype(f32)
    term_sum = tg_out.at[0]

    def await_sent(k):
        @pl.when(jnp.logical_not((y_lo == core) & (k == my_block)))
        def _():
            remote(
                tg_out.at[k], tg_in.at[0], gp_send.at[k], gp_recv.at[0], sibling
            ).wait_send()

    loop(0, PLANE, await_sent)
    term_sum[...] = sums.astype(bf16)

    def unit_of(v):
        apart = lax.rem(v - z + n, n)
        near = jnp.where(apart < half, 2 * apart, 2 * (n - apart) - 1)
        return jnp.where(apart == half, n - 1, near)

    def slots(g):
        nothing = jnp.zeros((16, 128), bf16)
        first, second = term_sum[unit_of(g)], term_sum[unit_of(ids[3, g])]
        tg_send[g, 0] = jnp.where(counts[g] == 0, nothing, first)
        tg_send[g, 1] = jnp.where(counts[g] == 2, second, nothing)

    loop(0, n, slots)

    def slot_copy(k):
        to = lax.rem(z + k, n)
        return remote(tg_send.at[to], tg_fin.at[z], gz_send.at[k], gz_recv.at[k], {"dp": to})

    loop(1, n, lambda k: slot_copy(k).start())
    tg_fin[z] = tg_send[z]

    for way in (0, 1):
        for p in range(4):
            reach = half if p in start_pieces(half, way) else half - 1
            loop(1, reach + 1, lambda d, way=way, p=p: ag_copy(way, d, p, 0).wait_send())
    loop(0, experts, lambda e: cross_copy(e).wait_send())

    def home(k):
        for w in (0, 1):
            home_copy(k, w).wait()

    loop(1, experts, home)
    for w in (0, 1):
        own_home(w).wait()
    loop(1, n, lambda k: slot_copy(k).wait())
    out_tokens[...] = tg_fin[...]


def finish_kernel(gate, up, out_gate, out_up, sems):
    pieces = sems.shape[1]
    size = gate.shape[0] // pieces
    for go in (True, False):
        for w, (src, dst) in enumerate(((gate, out_gate), (up, out_up))):
            for i in range(pieces):
                some = pl.ds(i * size, size)
                copy = pltpu.make_async_copy(src.at[some], dst.at[some], sems.at[w, i])
                copy.start() if go else copy.wait()


def local(tokens, upstream, router, counts, w_gate, w_up):
    n = lax.axis_size("dp")
    _, slots, seg_len, width = tokens.shape
    _, depth, blocks, cols = w_gate.shape
    experts = router.shape[2]
    half = n // 2
    hidden = 4 * cols
    vmem, smem, hbm = (
        pl.BlockSpec(memory_space=space) for space in (pltpu.VMEM, pltpu.SMEM, pl.ANY)
    )
    dma = pltpu.SemaphoreType.DMA
    home = jax.ShapeDtypeStruct((blocks, cols, depth), bf16)
    tg, gate_grad, up_grad = pl.pallas_call(
        functools.partial(kernel, n),
        out_shape=(jax.ShapeDtypeStruct((n, slots, 16, depth), bf16), home, home),
        in_specs=[smem, smem, hbm, hbm, hbm, vmem],
        out_specs=(vmem, hbm, hbm),
        scratch_shapes=[
            pltpu.SMEM((4, n), jnp.int32),
            pltpu.SMEM((n, experts), f32),
            pltpu.VMEM((2, experts, 2, cols, depth), bf16),
            pltpu.VMEM((n, slots, 16, depth), bf16),
            pltpu.VMEM((TILES, n, 16, depth), bf16),
            pltpu.VMEM((slots, ROWS, 512), bf16),
            pltpu.VMEM((slots, ROWS, 512), bf16),
            pltpu.VMEM((slots, ROWS, 512), bf16),
            pltpu.VMEM((n, 16, 512), bf16),
            pltpu.VMEM((n, 16, 512), bf16),
            pltpu.VMEM((ROWS, 512), bf16),
            pltpu.VMEM((n, hidden, depth), bf16),
            pltpu.VMEM((2, 2, ROWS, hidden), f32),
            pltpu.VMEM((2, half + 1, ROWS, hidden), bf16),
            pltpu.VMEM((n, ROWS, hidden), bf16),
            pltpu.VMEM((experts, hidden, depth), f32),
            pltpu.VMEM((2, ROWS, depth), bf16),
            pltpu.VMEM((PLANE, n, 16, depth), bf16),
            pltpu.VMEM((PLANE, n, 16, depth), bf16),
            pltpu.VMEM((n, slots, 16, depth), bf16),
            pltpu.VMEM((n, slots, 16, depth), bf16),
            pltpu.VMEM((experts, 2, cols, depth), bf16),
            pltpu.VMEM((experts, 2, cols, depth), bf16),
            pltpu.VMEM((experts, 2, cols, depth), bf16),
            dma((3,)),
            dma((experts, 2)), dma((experts, 2)),
            dma((experts, 2)), dma((experts, 2)),
            dma((n,)), dma((n,)),
            dma((2, PLANE)), dma((2, TILES)),
            dma((2,)),
            dma((TILES,)), dma((n,)),
            dma((n,)), dma((PLANE,)),
            dma((2, 4)), dma((2, half, 4)),
            dma((2, half, 4)), dma((2, half, 4)),
            dma((PLANE,)), dma((PLANE,)),
            dma((n,)), dma((n,)),
            dma((experts,)), dma((experts,)),
            dma((experts, 2)), dma((experts, 2)),
        ],
        compiler_params=pltpu.CompilerParams(
            collective_id=0, has_side_effects=True, vmem_limit_bytes=56 * 2**20
        ),
    )(
        counts,
        router.transpose(1, 2, 0),
        w_gate[0].transpose(1, 2, 0),
        w_up[0].transpose(1, 2, 0),
        tokens[0],
        upstream[0].transpose(0, 2, 1),
    )
    gate_grad, up_grad = pl.pallas_call(
        finish_kernel,
        out_shape=(home, home),
        in_specs=[vmem, vmem],
        out_specs=(hbm, hbm),
        scratch_shapes=[dma((2, 4))],
    )(gate_grad, up_grad)
    tokens_grad = tg[:, :, : seg_len // 32].transpose(1, 2, 0, 3).reshape(1, slots, -1, width)
    return (tokens_grad, gate_grad.transpose(2, 0, 1)[None], up_grad.transpose(2, 0, 1)[None])


def solution(mesh):
    shape = (mesh.shape["dp"], 2, mesh.shape["expert"] // 2, mesh.shape["tensor"] // 2, 2)
    fine = Mesh(mesh.devices.reshape(shape), ("dp", "y_lo", "x", "y_hi", "core"))
    tensor = ("y_hi", "core")
    weights = P(EXPERT, "dp", None, tensor)
    in_specs = (
        P("dp", None, None, None),
        P("dp", None, None, EXPERT + tensor),
        P(),
        P(),
        weights,
        weights,
    )
    out_specs = (P("dp", None, EXPERT + tensor, None), weights, weights)
    return jax.shard_map(local, mesh=fine, in_specs=in_specs, out_specs=out_specs, check_vma=False)
```

```python
import functools

import jax
import jax.numpy as jnp
from jax import lax
from jax.experimental import pallas as pl
from jax.experimental.pallas import tpu as pltpu
from jax.sharding import Mesh, PartitionSpec as P

MESH = pl.DeviceIdType.MESH
EXPERT = ("y_lo", "x")
PLANE = 16
ROWS = 176
TILES = 11
COLS = 224
PIECES = ((0, 48), (48, 48), (96, 48), (144, 32))
BATCHES = ((0, 3), (3, 13))
PARTS = ((0, 256), (256, 256), (512, 256), (768, 128))
NT = (((1,), (1,)), ((), ()))
TN = (((0,), (0,)), ((), ()))
f32, bf16 = jnp.float32, jnp.bfloat16


def loop(lo, hi, body):
    def step(i, carry):
        body(i)
        return carry

    lax.fori_loop(lo, hi, step, 0)


def kernel(
    n, counts, router, w_gate, w_up, tokens, upstream,
    out_tokens, out_gate, out_up,
    ids, rv, raw, zrecv, tokbuf, upsend, uprecv, upfull, up1, up2, upmoved,
    merged, contrib, inbox, spread, acc,
    term, tg_out, tg_in, tg_send, tg_fin, sib_out, sib_in, wg_out,
    local_sem, w_send, w_recv, s_send, s_recv, tz_send, tz_recv, tp_send, tp_recv,
    us_sem, u1_send, u1_recv, u2_send, u2_recv,
    rs_send, rs_recv, ag_send, ag_recv,
    gp_send, gp_recv, gz_send, gz_recv, x_send, x_recv, e_send, e_recv,
):
    z = lax.axis_index("dp")
    y_lo, x, y_hi = lax.axis_index("y_lo"), lax.axis_index("x"), lax.axis_index("y_hi")
    core = lax.axis_index("core")
    expert = y_lo * 4 + x
    place = expert * 2 + y_hi
    half = n // 2
    experts = raw.shape[1]
    right, left = lax.rem(z + 1, n), lax.rem(z + n - 1, n)
    towards = (right, left)

    def on_plane(q, c):
        return {"y_lo": q // 8, "x": lax.rem(q // 2, 4), "y_hi": lax.rem(q, 2), "core": c}

    def on_expert(e):
        return {"y_lo": e // 4, "x": lax.rem(e, 4)}

    sibling = {"core": 1 - core}

    def remote(src, dst, send, recv, where):
        return pltpu.make_async_remote_copy(
            src_ref=src, dst_ref=dst, send_sem=send, recv_sem=recv,
            device_id=where, device_id_type=MESH,
        )

    def ahead(way, d):
        return lax.rem(z + d, n) if way == 0 else lax.rem(z + n - d, n)

    def behind(way, d):
        return ahead(1 - way, d)

    barrier = pltpu.get_barrier_semaphore()

    def greet(where):
        pl.semaphore_signal(barrier, inc=1, device_id=where, device_id_type=MESH)

    greet(sibling)
    loop(1, n, lambda k: greet({"dp": lax.rem(z + k, n)}))

    def greet_chip(k):
        q = lax.rem(place + k, PLANE)
        greet(on_plane(q, 0))
        greet(on_plane(q, 1))

    loop(1, PLANE, greet_chip)
    pl.semaphore_wait(barrier, 1 + (n - 1) + 2 * (PLANE - 1))

    tile = lax.rem(place + TILES * core, PLANE)
    serves = tile < TILES

    def token_block(to):
        rows = pl.ds(pl.multiple_of(core * ROWS + tile * 16, 16), 16)
        return tokens.at[:, rows, pl.ds(pl.multiple_of(to * 128, 128), 128)]

    def token_copy(k):
        to = lax.rem(z + k, n)
        return remote(token_block(to), zrecv.at[z], tz_send.at[k], tz_recv.at[k], {"dp": to})

    own_tokens = pltpu.make_async_copy(token_block(z), zrecv.at[z], local_sem.at[2])

    @pl.when(serves)
    def _():
        loop(1, n, lambda k: token_copy(k).start())
        own_tokens.start()

    stored = (w_gate, w_up)

    def weight_copy(k, w):
        to = lax.rem(expert + k, experts)
        return remote(
            stored[w].at[to], raw.at[core, expert, w], w_send.at[k, w], w_recv.at[k, w], on_expert(to)
        )

    def own_weights(w):
        return pltpu.make_async_copy(stored[w].at[expert], raw.at[core, expert, w], local_sem.at[w])

    for w in (0, 1):
        own_weights(w).start()

    def send_weights(k):
        for w in (0, 1):
            weight_copy(k, w).start()

    loop(1, experts, send_weights)

    row = lax.broadcasted_iota(jnp.int32, (ROWS, 2 * ROWS), 0)
    col = lax.broadcasted_iota(jnp.int32, (ROWS, 2 * ROWS), 1)
    unit = lax.broadcasted_iota(jnp.int32, (COLS, 512), 0)
    lane = lax.broadcasted_iota(jnp.int32, (COLS, 512), 1)
    tail = unit >= 192
    spot = jnp.where(
        tail, unit + (192 + 32 * core), (unit >> 6) * 128 + (unit & 63) + 64 * core
    )
    put = ((lane == spot) | (tail & (lane == spot + 64))).astype(f32).astype(bf16)

    def upstream_rows(k, which):
        pick = (col == row + ROWS * which).astype(f32).astype(bf16)
        turned = lax.dot_general(pick, upstream[k], NT, preferred_element_type=f32)
        return jnp.dot(turned.astype(bf16), put, preferred_element_type=f32).astype(bf16)

    for k in (0, 1):
        upsend[k] = upstream_rows(k, 1 - core)
    up_swap = remote(upsend, uprecv, us_sem.at[0], us_sem.at[1], sibling)
    up_swap.start()

    def ranks(g, carry):
        empties, doubles = carry
        ids[0, g] = empties
        ids[1, g] = doubles
        held = counts[g]
        return (
            empties + jnp.where(held == 0, 1, 0),
            doubles + jnp.where(held == 2, 1, 0),
        )

    lax.fori_loop(0, n, ranks, (jnp.int32(0), jnp.int32(0)))

    def pair(d):
        partner, helper = jnp.int32(0), jnp.int32(0)
        for g in range(n):
            lends = (counts[d] == 0) & (counts[g] == 2) & (ids[0, d] == ids[1, g])
            partner = partner + jnp.where(lends, g, 0)
            helps = (counts[g] == 0) & (counts[d] == 2) & (ids[0, g] == ids[1, d])
            helper = helper + jnp.where(helps, g, 0)
        ids[2, d] = partner
        ids[3, d] = helper
        slot = jnp.where(counts[d] == 0, 1, 0)
        group = jnp.where(counts[d] == 0, partner, d)
        for e in range(experts):
            rv[d, e] = router[slot, e, group]

    loop(0, n, pair)

    for k in (0, 1):
        upfull[k] = upstream_rows(k, core)

    up_swap.wait()
    for k in (0, 1):
        upfull[k] = (upfull[k].astype(f32) + uprecv[k].astype(f32)).astype(bf16)

    def keeper(i):
        return lax.rem(i + half * core, n)

    kept = lax.rem(z + half * core, n)
    keeps = kept < TILES

    def scatter_copy(i):
        rows = pl.ds(pl.multiple_of(i * 16, 16), 16)
        return remote(
            upfull.at[1, rows], up1.at[z], u1_send.at[i], u1_recv.at[z], {"dp": keeper(i)}
        )

    def scatter(i):
        @pl.when(keeper(i) != z)
        def _():
            scatter_copy(i).start()

        @pl.when(keeper(i) == z)
        def _():
            up1[z] = upfull[1, pl.ds(pl.multiple_of(i * 16, 16), 16)]

    loop(0, TILES, scatter)

    def order(v):
        return lax.rem(v - z + half + 1 + n, n)

    def tile_copy(k, b):
        to = lax.rem(place + k, PLANE)
        some = pl.ds(*BATCHES[b])
        return remote(
            tokbuf.at[tile, some], tokbuf.at[tile, some],
            tp_send.at[b, k], tp_recv.at[b, tile], on_plane(to, core),
        )

    @pl.when(serves)
    def _():
        loop(1, n, lambda k: token_copy(k).wait_recv())
        own_tokens.wait()

        def choose(v):
            lent, own = zrecv[ids[2, v], 1], zrecv[v, 0]
            tokbuf[tile, order(v)] = jnp.where(counts[v] == 0, lent, own)

        loop(0, n, choose)
        loop(1, PLANE, lambda k: tile_copy(k, 0).start())

    def pass_block(e, w):
        return remote(
            raw.at[core, e, w], raw.at[core, e, w], s_send.at[e, w], s_recv.at[e, w], sibling
        )

    for w in (0, 1):
        own_weights(w).wait()
        pass_block(expert, w).start()

    def pass_weights(k):
        e = lax.rem(expert + experts - k, experts)
        for w in (0, 1):
            remote(
                stored[w].at[0], raw.at[core, e, w], w_send.at[k, w], w_recv.at[k, w], sibling
            ).wait_recv()
            pass_block(e, w).start()

    loop(1, experts, pass_weights)


    def gather_copy(k):
        to = lax.rem(z + k, n)
        rows = pl.ds(pl.multiple_of(kept * 16, 16), 16)
        return remote(up2.at[to], upmoved.at[rows], u2_send.at[k], u2_recv.at[kept], {"dp": to})

    @pl.when(keeps)
    def _():
        def await_scatter(k):
            g = lax.rem(z + k, n)
            remote(
                up2.at[0], up1.at[g], u1_send.at[0], u1_recv.at[g], {"dp": right}
            ).wait_recv()

        loop(1, n, await_scatter)

        def lend(d):
            up2[d] = up1[ids[2, d]]

        loop(0, n, lend)
        loop(1, n, lambda k: gather_copy(k).start())
        upmoved[pl.ds(pl.multiple_of(kept * 16, 16), 16)] = up2[z]

    def await_weights(e):
        for w in (0, 1):
            remote(
                raw.at[core, e, w], raw.at[1 - core, e, w], s_send.at[e, w], s_recv.at[e, w], sibling
            ).wait_recv()

    loop(0, experts, await_weights)

    def await_tiles(b):
        some = pl.ds(*BATCHES[b])

        def await_tile(t):
            @pl.when(t != tile)
            def _():
                remote(
                    tokbuf.at[t, some], tokbuf.at[t, some], tp_send.at[b, 0], tp_recv.at[b, t], sibling
                ).wait_recv()

        loop(0, TILES, await_tile)

    await_tiles(0)

    def merge(v):
        weights = [rv[v, e] for e in range(experts)]

        def block(s, w, src, dst):
            total = weights[0] * raw[s, 0, w, src].astype(f32)
            for e in range(1, experts):
                total = total + weights[e] * raw[s, e, w, src].astype(f32)
            merged[v, dst] = total.astype(bf16)

        def tiles(q):
            for s in (0, 1):
                for w in (0, 1):
                    block(
                        s,
                        w,
                        pl.ds(pl.multiple_of(q * 64, 64), 64),
                        pl.ds(pl.multiple_of(w * 512 + q * 128 + s * 64, 64), 64),
                    )

        loop(0, 3, tiles)
        for s in (0, 1):
            for w in (0, 1):
                block(s, w, pl.ds(192, 32), pl.ds(384 + w * 64 + s * 32, 32))

    def tok(v):
        return tokbuf[:, order(v)].reshape(ROWS, 128)

    def partial(v):
        return lax.dot_general(tok(v), merged[v], NT, preferred_element_type=f32)

    def rs_copy(way, d, p):
        rows = pl.ds(*PIECES[p])
        return remote(
            inbox.at[way, d, rows], inbox.at[way, d - 1, rows],
            rs_send.at[way, p], rs_recv.at[way, d - 1, p], {"dp": towards[way]},
        )

    def ag_copy(way, d, p, v):
        rows = pl.ds(*PIECES[p])
        return remote(
            spread.at[v, rows], spread.at[v, rows],
            ag_send.at[way, d - 1, p], ag_recv.at[way, d - 1, p], {"dp": towards[way]},
        )

    def start_pieces(d, way):
        longer = (0, 1) if way == 0 else (2, 3)
        return longer if d == half else tuple(p for p in range(4) if p not in longer)

    far = ahead(0, half)
    merge(far)
    first = partial(far).astype(bf16)
    for way in (0, 1):
        for p in start_pieces(half, way):
            at, size = PIECES[p]
            inbox[way, half, at : at + size] = first[at : at + size]
            rs_copy(way, half, p).start()

    @pl.when(serves)
    def _():
        loop(1, PLANE, lambda k: tile_copy(k, 1).start())

    for way in (0, 1):
        v = ahead(way, half - 1)
        merge(v)
        contrib[(half - 1) % 2, way] = partial(v)
        for p in start_pieces(half - 1, way):
            rows = pl.ds(*PIECES[p])
            inbox[way, half - 1, rows] = contrib[(half - 1) % 2, way, rows].astype(bf16)
            rs_copy(way, half - 1, p).start()
    await_tiles(1)

    def pass_on(way, d, p):
        rows = pl.ds(*PIECES[p])
        rs_copy(way, d + 1, p).wait_recv()
        total = inbox[way, d, rows].astype(f32) + contrib[lax.rem(d, 2), way, rows]
        inbox[way, d, rows] = total.astype(bf16)
        rs_copy(way, d, p).start()

    def prepare(d, i):
        way, second = i // 2, i % 2
        v = ahead(way, d)
        if second:
            contrib[lax.rem(d, 2), way] = partial(v)
        else:
            merge(v)

    for i in range(4):
        if i < 2:
            pass_on(0, half - 1, start_pieces(half, 0)[i])
            pass_on(1, half - 1, start_pieces(half, 1)[i])
        prepare(half - 2, i)

    def rs_step(i):
        d = half - 2 - i
        for j, (up, down) in enumerate(((2, 0), (3, 1), (0, 2), (1, 3))):
            pass_on(0, d, up)
            pass_on(1, d, down)
            prepare(d - 1, j)

    loop(0, half - 2, rs_step)

    def await_gather(i):
        @pl.when(i != kept)
        def _():
            rows = pl.ds(pl.multiple_of(i * 16, 16), 16)
            remote(
                up2.at[0], upmoved.at[rows], u2_send.at[0], u2_recv.at[i], {"dp": right}
            ).wait_recv()

    loop(0, TILES, await_gather)

    def gate_part(gate, up, flowing):
        s = jax.nn.sigmoid(gate)
        return (flowing * up * s * (1.0 + gate * (1.0 - s))).astype(bf16)

    def up_part(gate, flowing):
        return (flowing * gate * jax.nn.sigmoid(gate)).astype(bf16)

    for p in range(4):
        rows = pl.ds(*PIECES[p])
        for way in (0, 1):
            rs_copy(way, 1, p).wait_recv()
        pre = inbox[0, 0, rows].astype(f32) + inbox[1, 0, rows].astype(f32) + contrib[0, 0, rows]
        flowing = jnp.where(counts[z] == 0, upmoved[rows], upfull[0, rows]).astype(f32)
        gate, mixed, up = pre[:, :384], pre[:, 384:512], pre[:, 512:]
        spread[z, rows, :384] = gate_part(gate, up, flowing[:, :384])
        spread[z, rows, 512:] = up_part(gate, flowing[:, :384])
        low = lax.broadcasted_iota(jnp.int32, mixed.shape, 1) < 64
        rolled = pltpu.roll(mixed, 64, 1)
        gate, up = jnp.where(low, mixed, rolled), jnp.where(low, rolled, mixed)
        spread[z, rows, 384:512] = jnp.where(
            low, gate_part(gate, up, flowing[:, 384:]), up_part(gate, flowing[:, 384:])
        )
        for way in (0, 1):
            ag_copy(way, 1, p, z).start()

    acc[...] = jnp.zeros_like(acc)

    wide = lax.broadcasted_iota(jnp.int32, (PLANE * 16, ROWS), 0)
    slim = lax.broadcasted_iota(jnp.int32, (PLANE * 16, ROWS), 1)
    spare = (wide & 15) < TILES
    widen = (spare & (slim == (wide >> 4) * TILES + (wide & 15))).astype(f32).astype(bf16)
    my_block = x * 4 + y_hi * 2 + core

    def back(owners, i, unit):
        back_tokens(owners, i, unit)
        back_weights(owners, i)
        if i == 3:
            send_terms(unit, len(owners))

    def back_tokens(owners, i, unit):
        rows = pl.ds(*PIECES[i])
        for j, v in enumerate(owners):
            term[j, rows] = jnp.dot(
                spread[v, rows], merged[v], preferred_element_type=f32
            ).astype(bf16)
            if i == 3:
                blocks = jnp.dot(widen, term[j], preferred_element_type=f32).astype(bf16)
                tg_out[:, unit + j] = blocks.reshape(PLANE, 16, 128)

    def back_weights(owners, i):
        hidden = pl.ds(*PARTS[i])
        terms = [
            lax.dot_general(spread[v, :, hidden], tok(v), TN, preferred_element_type=f32)
            for v in owners
        ]
        for e in range(experts):
            total = acc[e, hidden]
            for v, t in zip(owners, terms):
                total = total + rv[v, e] * t
            acc[e, hidden] = total

    def term_copy(k, units):
        where = {"y_lo": core, "x": k // 4, "y_hi": lax.rem(k // 2, 2), "core": lax.rem(k, 2)}
        return remote(
            tg_out.at[k, units], tg_in.at[place, units], gp_send.at[k], gp_recv.at[place], where
        )

    def send_terms(unit, count):
        units = pl.ds(unit, count)

        def send(k):
            here = (y_lo == core) & (k == my_block)

            @pl.when(here)
            def _():
                tg_in[place, units] = tg_out[k, units]

            @pl.when(jnp.logical_not(here))
            def _():
                term_copy(k, units).start()

        loop(0, PLANE, send)

    def receive(way, d, p):
        ag_copy(way, d, p, behind(way, d)).wait_recv()

    def forward(way, d, p):
        ag_copy(way, d + 1, p, behind(way, d)).start()

    def ag_step(d, owners, last, unit):
        for p in range(4):
            for way in (0, 1):
                receive(way, d, p)
                if not last or p in start_pieces(half, way):
                    forward(way, d, p)
            back(owners, p, unit)

    ag_step(1, (z,), False, 0)
    loop(
        2,
        half - 1,
        lambda d: ag_step(d, (behind(0, d - 1), behind(1, d - 1)), False, 2 * d - 3),
    )
    ag_step(half - 1, (behind(0, half - 2), behind(1, half - 2)), True, n - 5)
    for i in range(4):
        back((behind(0, half - 1), behind(1, half - 1)), i, n - 3)

    for way in (0, 1):
        for p in range(4):
            reach = half if p in start_pieces(half, way) else half - 1
            started = inbox.at[way, pl.ds(1, reach), pl.ds(*PIECES[p])]
            remote(
                started, started, rs_send.at[way, p], rs_recv.at[way, 0, p], sibling
            ).wait_send()

    @pl.when(serves)
    def _():
        loop(1, n, lambda k: token_copy(k).wait_send())
        for b in (0, 1):
            loop(1, PLANE, lambda k, b=b: tile_copy(k, b).wait_send())

    def weights_sent(k):
        for w in (0, 1):
            weight_copy(k, w).wait_send()

    loop(1, experts, weights_sent)

    def passed(e):
        for w in (0, 1):
            pass_block(e, w).wait_send()

    loop(0, experts, passed)

    def scattered(i):
        @pl.when(keeper(i) != z)
        def _():
            scatter_copy(i).wait_send()

    loop(0, TILES, scattered)

    @pl.when(keeps)
    def _():
        loop(1, n, lambda k: gather_copy(k).wait_send())

    for way in (0, 1):
        for p in start_pieces(half, way):
            receive(way, half, p)
    for i in range(4):
        back_weights((far,), i)

    other = 1 - core

    def units_of(w, s):
        for q in range(3):
            yield q * 64, 64, pl.ds(pl.multiple_of(w * 512 + q * 128 + s * 64, 64), 64)
        yield 192, 32, pl.ds(pl.multiple_of(384 + w * 64 + s * 32, 32), 32)

    def cross_copy(e):
        return remote(sib_out.at[e], sib_in.at[e], x_send.at[e], x_recv.at[e], sibling)

    def cross(e):
        for w in (0, 1):
            for at, size, hidden in units_of(w, other):
                sib_out[e, w, at : at + size] = acc[e, hidden].astype(bf16)
        cross_copy(e).start()

    loop(1, experts + 1, lambda k: cross(lax.rem(expert + k, experts)))
    for i in range(4):
        back_tokens((far,), i, n - 1)
    send_terms(n - 1, 1)

    outs = (out_gate, out_up)

    def home_copy(k, w):
        to = lax.rem(expert + k, experts)
        return remote(
            wg_out.at[to, w], outs[w].at[expert], e_send.at[k, w], e_recv.at[k, w], on_expert(to)
        )

    def own_home(w):
        return pltpu.make_async_copy(wg_out.at[expert, w], outs[w].at[expert], local_sem.at[w])

    def settle(k):
        e = lax.rem(expert + k, experts)
        cross_copy(e).wait_recv()
        for w in (0, 1):
            for at, size, hidden in units_of(w, core):
                total = acc[e, hidden] + sib_in[e, w, at : at + size].astype(f32)
                wg_out[e, w, at : at + size] = total.astype(bf16)

        @pl.when(k < experts)
        def _():
            for w in (0, 1):
                home_copy(k, w).start()

    loop(1, experts + 1, settle)
    for w in (0, 1):
        own_home(w).start()

    def await_terms(q):
        @pl.when(jnp.logical_not((y_lo == core) & (q == place)))
        def _():
            remote(
                tg_in.at[q], tg_in.at[q], gp_send.at[0], gp_recv.at[q], sibling
            ).wait_recv()

    loop(0, PLANE, await_terms)
    sums = tg_in[0].astype(f32)
    for q in range(1, PLANE):
        sums = sums + tg_in[q].astype(f32)
    term_sum = tg_out.at[0]

    def await_sent(k):
        @pl.when(jnp.logical_not((y_lo == core) & (k == my_block)))
        def _():
            remote(
                tg_out.at[k], tg_in.at[0], gp_send.at[k], gp_recv.at[0], sibling
            ).wait_send()

    loop(0, PLANE, await_sent)
    term_sum[...] = sums.astype(bf16)

    def unit_of(v):
        apart = lax.rem(v - z + n, n)
        near = jnp.where(apart < half, 2 * apart, 2 * (n - apart) - 1)
        return jnp.where(apart == half, n - 1, near)

    def slots(g):
        nothing = jnp.zeros((16, 128), bf16)
        first, second = term_sum[unit_of(g)], term_sum[unit_of(ids[3, g])]
        tg_send[g, 0] = jnp.where(counts[g] == 0, nothing, first)
        tg_send[g, 1] = jnp.where(counts[g] == 2, second, nothing)

    loop(0, n, slots)

    def slot_copy(k):
        to = lax.rem(z + k, n)
        return remote(tg_send.at[to], tg_fin.at[z], gz_send.at[k], gz_recv.at[k], {"dp": to})

    loop(1, n, lambda k: slot_copy(k).start())
    tg_fin[z] = tg_send[z]

    for way in (0, 1):
        for p in range(4):
            reach = half if p in start_pieces(half, way) else half - 1
            loop(1, reach + 1, lambda d, way=way, p=p: ag_copy(way, d, p, 0).wait_send())
    loop(0, experts, lambda e: cross_copy(e).wait_send())

    def home(k):
        for w in (0, 1):
            home_copy(k, w).wait()

    loop(1, experts, home)
    for w in (0, 1):
        own_home(w).wait()
    loop(1, n, lambda k: slot_copy(k).wait())
    out_tokens[...] = tg_fin[...]


def finish_kernel(gate, up, out_gate, out_up, sems):
    pieces = sems.shape[1]
    size = gate.shape[0] // pieces
    for go in (True, False):
        for w, (src, dst) in enumerate(((gate, out_gate), (up, out_up))):
            for i in range(pieces):
                some = pl.ds(i * size, size)
                copy = pltpu.make_async_copy(src.at[some], dst.at[some], sems.at[w, i])
                copy.start() if go else copy.wait()


def local(tokens, upstream, router, counts, w_gate, w_up):
    n = lax.axis_size("dp")
    _, slots, seg_len, width = tokens.shape
    _, depth, blocks, cols = w_gate.shape
    experts = router.shape[2]
    half = n // 2
    hidden = 4 * cols
    vmem, smem, hbm = (
        pl.BlockSpec(memory_space=space) for space in (pltpu.VMEM, pltpu.SMEM, pl.ANY)
    )
    dma = pltpu.SemaphoreType.DMA
    home = jax.ShapeDtypeStruct((blocks, cols, depth), bf16)
    tg, gate_grad, up_grad = pl.pallas_call(
        functools.partial(kernel, n),
        out_shape=(jax.ShapeDtypeStruct((n, slots, 16, depth), bf16), home, home),
        in_specs=[smem, smem, hbm, hbm, hbm, vmem],
        out_specs=(vmem, hbm, hbm),
        scratch_shapes=[
            pltpu.SMEM((4, n), jnp.int32),
            pltpu.SMEM((n, experts), f32),
            pltpu.VMEM((2, experts, 2, cols, depth), bf16),
            pltpu.VMEM((n, slots, 16, depth), bf16),
            pltpu.VMEM((TILES, n, 16, depth), bf16),
            pltpu.VMEM((slots, ROWS, 512), bf16),
            pltpu.VMEM((slots, ROWS, 512), bf16),
            pltpu.VMEM((slots, ROWS, 512), bf16),
            pltpu.VMEM((n, 16, 512), bf16),
            pltpu.VMEM((n, 16, 512), bf16),
            pltpu.VMEM((ROWS, 512), bf16),
            pltpu.VMEM((n, hidden, depth), bf16),
            pltpu.VMEM((2, 2, ROWS, hidden), f32),
            pltpu.VMEM((2, half + 1, ROWS, hidden), bf16),
            pltpu.VMEM((n, ROWS, hidden), bf16),
            pltpu.VMEM((experts, hidden, depth), f32),
            pltpu.VMEM((2, ROWS, depth), bf16),
            pltpu.VMEM((PLANE, n, 16, depth), bf16),
            pltpu.VMEM((PLANE, n, 16, depth), bf16),
            pltpu.VMEM((n, slots, 16, depth), bf16),
            pltpu.VMEM((n, slots, 16, depth), bf16),
            pltpu.VMEM((experts, 2, cols, depth), bf16),
            pltpu.VMEM((experts, 2, cols, depth), bf16),
            pltpu.VMEM((experts, 2, cols, depth), bf16),
            dma((3,)),
            dma((experts, 2)), dma((experts, 2)),
            dma((experts, 2)), dma((experts, 2)),
            dma((n,)), dma((n,)),
            dma((2, PLANE)), dma((2, TILES)),
            dma((2,)),
            dma((TILES,)), dma((n,)),
            dma((n,)), dma((PLANE,)),
            dma((2, 4)), dma((2, half, 4)),
            dma((2, half, 4)), dma((2, half, 4)),
            dma((PLANE,)), dma((PLANE,)),
            dma((n,)), dma((n,)),
            dma((experts,)), dma((experts,)),
            dma((experts, 2)), dma((experts, 2)),
        ],
        compiler_params=pltpu.CompilerParams(
            collective_id=0, has_side_effects=True, vmem_limit_bytes=56 * 2**20
        ),
    )(
        counts,
        router.transpose(1, 2, 0),
        w_gate[0].transpose(1, 2, 0),
        w_up[0].transpose(1, 2, 0),
        tokens[0],
        upstream[0].transpose(0, 2, 1),
    )
    gate_grad, up_grad = pl.pallas_call(
        finish_kernel,
        out_shape=(home, home),
        in_specs=[vmem, vmem],
        out_specs=(hbm, hbm),
        scratch_shapes=[dma((2, 4))],
    )(gate_grad, up_grad)
    tokens_grad = tg[:, :, : seg_len // 32].transpose(1, 2, 0, 3).reshape(1, slots, -1, width)
    return (tokens_grad, gate_grad.transpose(2, 0, 1)[None], up_grad.transpose(2, 0, 1)[None])


def solution(mesh):
    shape = (mesh.shape["dp"], 2, mesh.shape["expert"] // 2, mesh.shape["tensor"] // 2, 2)
    fine = Mesh(mesh.devices.reshape(shape), ("dp", "y_lo", "x", "y_hi", "core"))
    tensor = ("y_hi", "core")
    weights = P(EXPERT, "dp", None, tensor)
    in_specs = (
        P("dp", None, None, None),
        P("dp", None, None, EXPERT + tensor),
        P(),
        P(),
        weights,
        weights,
    )
    out_specs = (P("dp", None, EXPERT + tensor, None), weights, weights)
    return jax.shard_map(local, mesh=fine, in_specs=in_specs, out_specs=out_specs, check_vma=False)
```
